32 devices in a mesh: dom: 8 (over z, y), brick: 4 (over x, core).
Axes of the slice: x: 2, y: 2, z: 4, core: 2. Of those that a mesh axis runs over, the one named last changes fastest.
Arguments:
- features: bfloat16 [65536, 256], P(('dom', 'brick')), may hold values from -6 to 6
- elem_owner: int32 [65536, 1], P(('dom', 'brick')), may hold values from 0 to 31; in each aligned block of 2048 rows (0 to 2047, 2048 to 4095, ...) at most 128 rows name the same one
- elem_voxel: int32 [65536], P(('dom', 'brick')), may hold values from 0 to 16383
- w_first: bfloat16 [256, 256], replicated, may hold values from -0.375 to 0.375
- b_first: float32 [256], replicated, may hold values from -3 to 3
- w_conv: bfloat16 [3, 3, 3, 256, 128], replicated, may hold values from -0.078125 to 0.078125
- cotangent: bfloat16 [8, 16, 16, 32, 128], P('dom', None, None, 'brick'), may hold values from -6 to 6
Outputs:
- volume_out: bfloat16 [8, 16, 16, 32, 128], P('dom', None, None, 'brick')
- conv_grad: float32 [3, 3, 3, 256, 128], replicated
- w_first_grad: float32 [256, 256], replicated
- b_first_grad: float32 [256], replicated
The draws below stay inside these ranges and needn't reach their ends.
Inputs may be any that keep to these rules, and one draw needn't show every extreme that they name: `elem_owner`: within the rows of one device, at most 128 rows name the same owner.
All inputs are finite; a program needn't handle non-finite values.
Results may differ from the reference program's by a relative error of at most 0.0065.
Values may be sent and summed in bfloat16 or wider, within the bound.
No kernel may reach another device: no remote copies, remote signals or barrier semaphores. Data moves between devices by JAX's collectives and lax.ppermute only.
A program may use at most 128 MiB of HBM per device.

```python
import math
import jax
import jax.numpy as jnp
import numpy as np
from jax import lax

C = 256
CO = 128
BX = 32
BY = 32
SZ = 16
E_DEV = 2048
ELEMS = 65536
CAP = 128
VOXS = 16384
BZ = 64
BRICKS = 8
OUT_CELLS = 65536
DEVICES = 32


def place_ends(entries, key, low, high):
    shape = entries.shape
    index_at = [jax.random.randint(jax.random.fold_in(key, axis), (), 0, shape[axis]) for axis in range(len(shape))]
    entries = entries.at[tuple(index_at)].set(low)
    longest = shape.index(max(shape))
    index_at[longest] = (index_at[longest] + 1) % shape[longest]
    return entries.at[tuple(index_at)].set(high)


def shard_levels(key, shape, split, low, top_value):
    loudness = 1.0
    for axis_at, shards_of in split:
        steps = jax.random.uniform(jax.random.fold_in(jax.random.fold_in(key, 6), axis_at), (shards_of,), jnp.float32, low / len(split), top_value / len(split))
        loudness = loudness * jnp.repeat(jnp.exp(steps), shape[axis_at] // shards_of).reshape((-1,) + (1,) * (len(shape) - 1 - axis_at))
    return loudness


def assign_block(key, own, number, rows, amount, top, reach, lean):
    ranking = jax.random.permutation(key, amount)
    crowded, ordinary = shares(amount, rows * top, reach, lean, True), shares(amount, rows * top, reach, lean, False)
    places = jnp.arange(amount)

    def named(tallies, offset_by):
        used = int((tallies > 0).sum())
        fixed = max(1, used // 4)
        passed = fixed + (places - fixed + offset_by * (used - fixed)) % max(1, amount - fixed)
        return jnp.zeros((amount,), jnp.int32).at[ranking[jnp.where(places < fixed, places, passed)]].set(jnp.asarray(tallies, jnp.int32))

    tallies = jnp.where(number % 4 == 0, named(crowded, number // 4), named(ordinary, number - number // 4 - 1))
    mixed = jax.random.permutation(jax.random.fold_in(own, 3), amount)
    giver, taker = mixed[0:amount // 2 * 2:2], mixed[1:amount // 2 * 2:2]
    room = jnp.minimum(tallies[giver] - 1, reach - tallies[taker]) // 2
    room = jnp.where((giver == ranking[0]) | (taker == ranking[0]) | (tallies[taker] == 0), 0, jnp.maximum(room, 0))
    passed = jax.random.randint(jax.random.fold_in(own, 4), (amount // 2,), 0, 1 << 20) % (room + 1)
    tallies = tallies.at[giver].add(-passed).at[taker].add(passed)
    labels = jnp.searchsorted(jnp.cumsum(tallies), jnp.arange(rows * top), side="right").astype(jnp.int32)
    table = labels.reshape(top, rows).T
    table = table[jax.random.permutation(jax.random.fold_in(own, 1), rows)]
    offset_by = jax.random.randint(jax.random.fold_in(own, 2), (rows, 1), 0, top)
    return jnp.take_along_axis(table, (jnp.arange(top)[None, :] + offset_by) % top, axis=1)


def shares(number_of, total, reach, slope, full):
    portions = [(1 << 20) // math.isqrt(rank ** slope) + 1 for rank in range(1, number_of + 1)]
    largest = reach if full else min(reach, max(-(-total // number_of), total * portions[0] // sum(portions)))
    least = 1 if total - largest >= number_of - 1 else 0
    holding, spare = [largest] + [least] * (number_of - 1), total - largest - least * (number_of - 1)
    while spare > 0:
        movable = [i for i in range(1, number_of) if holding[i] < largest] or [i for i in range(1, number_of) if holding[i] < reach]
        mass, left = sum([portions[i] for i in movable]), spare
        for i in movable:
            extra = min(reach - holding[i], max(1, left * portions[i] // mass), spare)
            holding[i] = holding[i] + extra
            spare = spare - extra
    return np.array(holding)


def bell_draw(stream_key, shape, scale, reach, cuts=(), kind=jnp.bfloat16):
    entries = scale * jax.random.normal(stream_key, shape, jnp.float32)
    if cuts:
        entries = entries * shard_levels(stream_key, shape, cuts, -0.22, 0.18)
    return jnp.clip(entries, -reach, reach).astype(kind)


def setup_inputs(seed: int = 0) -> dict:
    seeds = jax.random.split(jax.random.key(seed), 8)
    features = bell_draw(seeds[0], (ELEMS, C), 1.0, 6.0, ((0, 32),))
    elem_owner_keys = jax.random.split(jax.random.fold_in(seeds[1], 1), ELEMS // E_DEV)
    elem_owner_turns = jax.random.permutation(jax.random.fold_in(seeds[1], 3), ELEMS // E_DEV)
    elem_owner = jax.vmap(lambda own, number: assign_block(jax.random.fold_in(seeds[1], 2), own, number, E_DEV, DEVICES, 1, CAP, 2))(elem_owner_keys, elem_owner_turns).reshape((ELEMS, 1))
    elem_voxel = place_ends(jax.random.randint(seeds[2], (ELEMS,), 0, VOXS), jax.random.fold_in(seeds[2], 1), 0, VOXS - 1).astype(jnp.int32)
    w_first = bell_draw(seeds[3], (C, C), C ** -0.5, 0.375)
    b_first = bell_draw(seeds[4], (C,), 0.5, 3.0, (), jnp.float32)
    w_conv = bell_draw(seeds[5], (3, 3, 3, C, CO), (27 * C) ** -0.5, 0.078125)
    cotangent = bell_draw(seeds[6], (BRICKS, BX // 2, BY // 2, BZ // 2, CO), 1.0, 6.0, ((0, 8), (3, 4)))
    return dict(features=features, elem_owner=elem_owner, elem_voxel=elem_voxel, w_first=w_first, b_first=b_first, w_conv=w_conv, cotangent=cotangent)


def dsilu(pre):
    sig = jax.nn.sigmoid(pre)
    return sig * (1.0 + pre * (1.0 - sig))

def reference(features, elem_owner, elem_voxel, w_first, b_first, w_conv, cotangent):
    scale = 1.0 / math.sqrt(OUT_CELLS)
    pre = jnp.dot(features, w_first, preferred_element_type=jnp.float32) + b_first
    hidden = lax.optimization_barrier(jax.nn.silu(pre).astype(jnp.bfloat16))
    hidden_f = hidden.astype(jnp.float32)
    owner = elem_owner[:, 0]
    slabs = BZ // SZ
    brick_of = owner // slabs
    slab = owner % slabs
    plane = elem_voxel // SZ
    flat = plane * BZ + slab * SZ + elem_voxel % SZ
    cells = BX * BY * BZ
    kernel = w_conv.astype(jnp.float32)
    flipped = jnp.transpose(kernel[::-1, ::-1, ::-1], (0, 1, 2, 4, 3))
    dims = ('NDHWC', 'DHWIO', 'NDHWC')

    def per_brick(carry, index):
        grad_hidden, kernel_sum = carry
        inside = brick_of == index
        ids = jnp.where(inside, flat, cells).astype(jnp.int32)
        summed = jax.ops.segment_sum(hidden_f, ids, num_segments=cells + 1)[:cells]
        grid = summed.astype(jnp.bfloat16).reshape(BX, BY, BZ, C)
        padded = jnp.pad(grid, ((1, 0), (1, 0), (1, 0), (0, 0))).astype(jnp.float32)
        out = lax.conv_general_dilated(padded[None], kernel, (2, 2, 2), 'VALID', dimension_numbers=dims)[0]
        cot = lax.dynamic_index_in_dim(cotangent, index, 0, keepdims=False).astype(jnp.float32)
        wgrad = lax.conv_general_dilated(padded[None], cot[None], (1, 1, 1), 'VALID', rhs_dilation=(2, 2, 2), dimension_numbers=('CDHWN', 'IDHWO', 'NDHWC'))
        wgrad = jnp.transpose(wgrad, (1, 2, 3, 0, 4)) * scale
        dinput = lax.conv_general_dilated(cot[None], flipped, (1, 1, 1), [(2, 2), (2, 2), (2, 2)], lhs_dilation=(2, 2, 2), dimension_numbers=dims)[0] * scale
        grad_grid = dinput[1:, 1:, 1:, :].astype(jnp.bfloat16).reshape(cells, C)
        rows = grad_grid[jnp.clip(ids, 0, cells - 1)]
        grad_hidden = jnp.where(inside[:, None], rows, grad_hidden)
        return ((grad_hidden, kernel_sum + wgrad), out.astype(jnp.bfloat16))
    start = (jnp.zeros(hidden.shape, jnp.bfloat16), jnp.zeros((3, 3, 3, C, CO), jnp.float32))
    (grad_hidden, conv_grad), volume_out = lax.scan(per_brick, start, jnp.arange(BRICKS, dtype=jnp.int32))
    pre_grad = (grad_hidden.astype(jnp.float32) * dsilu(pre)).astype(jnp.bfloat16)
    w_first_grad = jnp.dot(features.T, pre_grad, preferred_element_type=jnp.float32)
    b_first_grad = lax.optimization_barrier(jnp.sum(pre_grad.astype(jnp.float32), axis=0))
    return (volume_out, conv_grad, w_first_grad, b_first_grad)
```

```python
import functools
import math

import jax
import jax.numpy as jnp
from jax import lax
from jax.experimental import pallas as pl
from jax.experimental.pallas import tpu as pltpu
from jax.sharding import PartitionSpec as P

BF16 = jnp.bfloat16
F32 = jnp.float32
LANES = 128
PAD = 16
VMEM = pl.BlockSpec(memory_space=pltpu.VMEM)
BIG = 60 * 2**20


def dot(a, b):
    return jnp.dot(a, b, preferred_element_type=F32)


def dot_nt(a, b):
    return lax.dot_general(a, b, (((1,), (1,)), ((), ())), preferred_element_type=F32)


def dot_tn(a, b):
    return lax.dot_general(a, b, (((0,), (0,)), ((), ())), preferred_element_type=F32)


def shifts_of(parity):
    return [s for s in range(8) if s & ~parity == 0]


def offset_of(parity, shift):
    index = 0
    for bit in (4, 2, 1):
        index = 3 * index + (1 if not parity & bit else 0 if shift & bit else 2)
    return index


def pack_kernel(group, cap, devices, target_ref, code_ref, feat_ref, out_ref, slot_ref, parts_ref):
    rows = feat_ref.shape[0]
    step = 2 * LANES

    @pl.when(pl.program_id(0) == 0)
    def _():
        before = lax.broadcasted_iota(jnp.int32, (step, step), 0) < lax.broadcasted_iota(
            jnp.int32, (step, step), 1
        )
        before = before.astype(F32).astype(BF16)
        device = lax.broadcasted_iota(jnp.int32, (devices, step), 0)
        seen = jnp.zeros((devices, 1), F32)
        for start in range(0, rows, step):
            here = (device == target_ref[:, start : start + step]).astype(F32)
            rank = dot(here.astype(BF16), before) + seen
            slot = jnp.sum(here * (rank + (device * cap).astype(F32)), axis=0, keepdims=True)
            slot_ref[:, start : start + step] = slot.astype(jnp.int32)
            seen = seen + jnp.sum(here, axis=1, keepdims=True)
        code = code_ref[...]
        kind = lax.broadcasted_iota(jnp.int32, (16, rows), 0)
        parts = jnp.where(kind == 0, (code >> 7) + 1, jnp.where(kind == 1, code & 127, 0))
        parts_ref[...] = parts.astype(F32).astype(BF16)

    first = pl.program_id(0) * (group * cap)
    place = lax.broadcasted_iota(jnp.int32, (group * cap, rows), 0) + first
    chosen = jnp.where(place == slot_ref[...], 1.0, 0.0).astype(BF16)
    packed = dot(chosen, feat_ref[...]).astype(BF16)
    voxels = dot_nt(parts_ref[...], chosen)
    for g in range(group):
        out_ref[g, :cap, :] = packed[g * cap : (g + 1) * cap]
        mine = voxels[:, g * cap : (g + 1) * cap]
        if cap < LANES:
            mine = jnp.concatenate([mine, jnp.zeros((16, LANES - cap), F32)], axis=1)
        both = jnp.concatenate([mine[0:1], mine[1:2]], axis=1)
        out_ref[g, cap:, :] = jnp.broadcast_to(both, (PAD, 2 * LANES)).astype(BF16)


def pack(target, code, features, cap, devices):
    rows, width = features.shape
    group = max(1, 512 // cap)
    return pl.pallas_call(
        functools.partial(pack_kernel, group, cap, devices),
        out_shape=jax.ShapeDtypeStruct((devices, cap + PAD, width), BF16),
        grid=(devices // group,),
        in_specs=[VMEM] * 3,
        out_specs=pl.BlockSpec((group, cap + PAD, width), lambda i: (i, 0, 0)),
        scratch_shapes=[pltpu.VMEM((1, rows), jnp.int32), pltpu.VMEM((16, rows), BF16)],
        compiler_params=pltpu.CompilerParams(vmem_limit_bytes=BIG),
        name="pack",
    )(target, code, features)


def prepare_kernel(dims, cot0_ref, cot1_ref, wide_ref, tall_ref):
    half_x, half_y, half_z = dims
    cells = half_x * half_y * half_z
    width = cot0_ref.shape[1]
    for shift in range(8):
        values = (cot1_ref if shift & 1 else cot0_ref)[...].astype(F32)
        if shift & 4:
            gap = half_y * half_z
            values = jnp.concatenate([values[gap:], jnp.zeros((gap, width), F32)], axis=0)
        if shift & 2:
            values = values.reshape(half_x, half_y * half_z, width)
            gone = jnp.zeros((half_x, half_z, width), F32)
            values = jnp.concatenate([values[:, half_z:], gone], axis=1).reshape(cells, width)
        wide_ref[:, shift * width : (shift + 1) * width] = values.astype(BF16)
        tall_ref[shift * width : (shift + 1) * width, :] = values.T.astype(BF16)


def prepare(cot0, cot1, dims):
    cells, width = cot0.shape
    return pl.pallas_call(
        functools.partial(prepare_kernel, dims),
        out_shape=(
            jax.ShapeDtypeStruct((cells, 8 * width), BF16),
            jax.ShapeDtypeStruct((8 * width, cells), BF16),
        ),
        in_specs=[VMEM] * 2,
        out_specs=(VMEM, VMEM),
        compiler_params=pltpu.CompilerParams(vmem_limit_bytes=BIG),
        name="prepare",
    )(cot0, cot1)


def read_codes(cap, vox_count, recv_ref, code_ref, smem_ref, sem):
    for s in range(recv_ref.shape[0]):
        both = recv_ref[s, cap:, :].astype(F32)[0:1]
        high, low = both[:, :LANES], both[:, LANES:]
        code = jnp.where(high > 0.5, (high - 1.0) * 128.0 + low, float(vox_count))
        code_ref[s : s + 1, :] = code.astype(jnp.int32)
    copy = pltpu.make_async_copy(code_ref, smem_ref, sem)
    copy.start()
    copy.wait()


def first_layer(features, w_ref, b_ref):
    return dot(features, w_ref[...]) + b_ref[...]


def per_row(sources, cap, smem_ref, body):
    unroll = 16

    def outer(s, _):
        def inner(i, _):
            for u in range(unroll):
                slot = i * unroll + u
                body(s * cap + slot, smem_ref[s, slot])
            return 0

        return lax.fori_loop(0, cap // unroll, inner, 0)

    lax.fori_loop(0, sources, outer, 0)


def forward_kernel(cap, recv_ref, w_ref, b_ref, tall_ref, grid_ref, grad_ref, sums, rows, codes, smem, sem):
    sources, _, width = recv_ref.shape
    vox_count = sums.shape[0] - 8
    cells = vox_count // 8
    out_width = tall_ref.shape[0] // 8
    read_codes(cap, vox_count, recv_ref, codes, smem, sem)

    def clear(i, _):
        sums[pl.ds(i * 512, 512)] = jnp.zeros((512, 2, LANES), F32)
        return 0

    lax.fori_loop(0, vox_count // 512, clear, 0)
    step = 512 // cap

    def layer(i, _):
        feats = recv_ref[pl.ds(i * step, step), :cap, :].reshape(step * cap, width)
        pre = first_layer(feats, w_ref, b_ref)
        hidden = (pre * jax.nn.sigmoid(pre)).astype(BF16).astype(F32)
        rows[pl.ds(i * step * cap, step * cap), 0, :] = hidden[:, :LANES]
        rows[pl.ds(i * step * cap, step * cap), 1, :] = hidden[:, LANES:]
        return 0

    lax.fori_loop(0, sources // step, layer, 0)

    def add(row, voxel):
        sums[voxel] = sums[voxel] + rows[row]

    per_row(sources, cap, smem, add)
    for parity in range(8):
        low = sums[parity * cells : (parity + 1) * cells, 0, :].astype(BF16)
        high = sums[parity * cells : (parity + 1) * cells, 1, :].astype(BF16)
        block = jnp.concatenate([low, high], axis=1)
        grid_ref[parity] = block
        shifts = shifts_of(parity)
        left = jnp.concatenate([tall_ref[s * out_width : (s + 1) * out_width, :] for s in shifts], axis=0)
        grads = dot(left, block)
        for at, s in enumerate(shifts):
            grad_ref[offset_of(parity, s)] = grads[at * out_width : (at + 1) * out_width].T.astype(BF16)


def forward(recv, w_first, b_first, tall, cap, vox_count):
    sources, _, width = recv.shape
    cells = vox_count // 8
    out_width = tall.shape[0] // 8
    return pl.pallas_call(
        functools.partial(forward_kernel, cap),
        out_shape=(
            jax.ShapeDtypeStruct((8, cells, width), BF16),
            jax.ShapeDtypeStruct((27, width, out_width), BF16),
        ),
        in_specs=[VMEM] * 4,
        out_specs=(VMEM, VMEM),
        scratch_shapes=[
            pltpu.VMEM((vox_count + 8, 2, LANES), F32),
            pltpu.VMEM((sources * cap, 2, LANES), F32),
            pltpu.VMEM((sources, LANES), jnp.int32),
            pltpu.SMEM((sources, LANES), jnp.int32),
            pltpu.SemaphoreType.DMA,
        ],
        compiler_params=pltpu.CompilerParams(vmem_limit_bytes=BIG),
        name="forward",
    )(recv, w_first, b_first, tall)


def backward_kernel(cap, scale, recv_ref, w_ref, b_ref, wide_ref, conv_ref, wgrad_ref, bgrad_ref, grads, rows, codes, smem, sem):
    sources, _, width = recv_ref.shape
    vox_count = grads.shape[0] - 8
    cells = vox_count // 8
    out_width = wide_ref.shape[1] // 8
    read_codes(cap, vox_count, recv_ref, codes, smem, sem)
    for parity in range(8):
        shifts = shifts_of(parity)
        left = jnp.concatenate([wide_ref[:, s * out_width : (s + 1) * out_width] for s in shifts], axis=1)
        right = jnp.concatenate([conv_ref[offset_of(parity, s)] for s in shifts], axis=1)
        block = (dot_nt(left, right) * scale).astype(BF16).astype(F32)
        grads[parity * cells : (parity + 1) * cells, 0, :] = block[:, :LANES]
        grads[parity * cells : (parity + 1) * cells, 1, :] = block[:, LANES:]
    grads[vox_count:] = jnp.zeros((8, 2, LANES), F32)

    def take(row, voxel):
        rows[row] = grads[voxel]

    per_row(sources, cap, smem, take)
    step = 512 // cap
    wgrad_ref[...] = jnp.zeros_like(wgrad_ref)
    bgrad_ref[...] = jnp.zeros_like(bgrad_ref)

    def layer(i, _):
        feats = recv_ref[pl.ds(i * step, step), :cap, :].reshape(step * cap, width)
        pre = first_layer(feats, w_ref, b_ref)
        low = rows[pl.ds(i * step * cap, step * cap), 0, :]
        high = rows[pl.ds(i * step * cap, step * cap), 1, :]
        sig = jax.nn.sigmoid(pre)
        slope = sig * (1.0 + pre * (1.0 - sig))
        pre_grad = (jnp.concatenate([low, high], axis=1) * slope).astype(BF16)
        wgrad_ref[...] += dot_tn(feats, pre_grad)
        bgrad_ref[...] += jnp.sum(pre_grad.astype(F32), axis=0, keepdims=True)
        return 0

    lax.fori_loop(0, sources // step, layer, 0)


def backward(recv, w_first, b_first, wide, w_conv, cap, vox_count, scale):
    sources, _, width = recv.shape
    return pl.pallas_call(
        functools.partial(backward_kernel, cap, scale),
        out_shape=(
            jax.ShapeDtypeStruct((width, width), F32),
            jax.ShapeDtypeStruct((1, width), F32),
        ),
        in_specs=[VMEM] * 5,
        out_specs=(VMEM, VMEM),
        scratch_shapes=[
            pltpu.VMEM((vox_count + 8, 2, LANES), F32),
            pltpu.VMEM((sources * cap, 2, LANES), F32),
            pltpu.VMEM((sources, LANES), jnp.int32),
            pltpu.SMEM((sources, LANES), jnp.int32),
            pltpu.SemaphoreType.DMA,
        ],
        compiler_params=pltpu.CompilerParams(vmem_limit_bytes=BIG),
        name="backward",
    )(recv, w_first, b_first, wide, w_conv)


def convolve_kernel(dims, grid_ref, conv_ref, out_ref, edge_ref, same, next_):
    half_x, half_y, half_z = dims
    cells = half_x * half_y * half_z
    plane = half_y * half_z
    width = conv_ref.shape[2]
    same[...] = jnp.zeros_like(same)
    next_[...] = jnp.zeros_like(next_)
    for parity in range(8):
        shifts = shifts_of(parity)
        right = jnp.concatenate([conv_ref[offset_of(parity, s)] for s in shifts], axis=1)
        product = dot(grid_ref[parity], right)
        for at, s in enumerate(shifts):
            part = product[:, at * width : (at + 1) * width].reshape(half_x, plane, width)
            dx = 1 if s & 4 else 0
            dy = half_z if s & 2 else 0
            total = next_ if s & 1 else same
            total[dx:, dy:, :] += part[: half_x - dx, : plane - dy, :]
    after = next_[...].reshape(cells, width)
    lowest = lax.broadcasted_iota(jnp.int32, (cells, width), 0) % half_z == 0
    out_ref[...] = same[...].reshape(cells, width) + jnp.where(lowest, 0.0, pltpu.roll(after, 1, 0))
    edge_ref[...] = after.reshape(cells // half_z, half_z, width)[:, half_z - 1, :]


def convolve(grid, w_conv, dims):
    half_x, half_y, half_z = dims
    cells = half_x * half_y * half_z
    width = w_conv.shape[2]
    return pl.pallas_call(
        functools.partial(convolve_kernel, dims),
        out_shape=(
            jax.ShapeDtypeStruct((cells, width), F32),
            jax.ShapeDtypeStruct((cells // half_z, width), F32),
        ),
        in_specs=[VMEM] * 2,
        out_specs=(VMEM, VMEM),
        scratch_shapes=[pltpu.VMEM((half_x, half_y * half_z, width), F32)] * 2,
        compiler_params=pltpu.CompilerParams(vmem_limit_bytes=BIG),
        name="convolve",
    )(grid, w_conv)


def passed_along(array, axis, by):
    size = lax.axis_size(axis)
    pairs = [(i, i + by) for i in range(size) if 0 <= i + by < size]
    return lax.ppermute(array, axis, pairs)


def exchange(array, axis, mask):
    return lax.ppermute(array, axis, [(i, i ^ mask) for i in range(lax.axis_size(axis))])


def halved(part, axis, mask):
    upper = lax.axis_index(axis) & mask != 0
    size = part.shape[0] // 2
    low, high = part[:size], part[size:]
    arrived = exchange(jnp.where(upper, low, high), axis, mask)
    return (jnp.where(upper, high, low).astype(F32) + arrived.astype(F32)).astype(BF16)


def doubled(part, axis, mask):
    upper = lax.axis_index(axis) & mask != 0
    arrived = exchange(part, axis, mask)
    return jnp.concatenate([jnp.where(upper, arrived, part), jnp.where(upper, part, arrived)], axis=0)


def bits(axis):
    return [(axis, 1 << i) for i in range(lax.axis_size(axis).bit_length() - 1)]


def summed(values):
    brick, dom = bits("brick"), bits("dom")
    first = brick[:1]
    orders = [brick[1:] + dom, dom[:1] + brick[1:] + dom[1:]]
    for axis, mask in first:
        values = halved(values, axis, mask)
    size = values.shape[0] // 2
    parts = [values[:size], values[size:]]
    for stage in range(len(orders[0])):
        parts = [halved(part, *order[stage]) for part, order in zip(parts, orders)]
    for stage in reversed(range(len(orders[0]))):
        parts = [doubled(part, *order[stage]) for part, order in zip(parts, orders)]
    values = jnp.concatenate(parts, axis=0)
    for axis, mask in reversed(first):
        values = doubled(values, axis, mask)
    return values


def shards(features, elem_owner, elem_voxel, w_first, b_first, w_conv, cotangent):
    devices = lax.axis_size("dom") * lax.axis_size("brick")
    rows, width = features.shape
    cap = 2 * rows // devices
    dims = cotangent.shape[1:4]
    half_x, half_y, half_z = dims
    cells = half_x * half_y * half_z
    vox_count = 8 * cells
    out_width = cotangent.shape[4]
    scale = 1.0 / math.sqrt(devices * cells)

    z = elem_voxel % (2 * half_z)
    y = elem_voxel // (2 * half_z) % (2 * half_y)
    x = elem_voxel // (4 * half_z * half_y)
    parity = (x % 2) * 4 + (y % 2) * 2 + z % 2
    code = parity * cells + ((x // 2) * half_y + y // 2) * half_z + z // 2
    packed = pack(elem_owner.reshape(1, rows), code.reshape(1, rows), features, cap, devices)
    recv = lax.all_to_all(packed, ("dom", "brick"), split_axis=0, concat_axis=0, tiled=True)

    cot = cotangent[0]
    upper = passed_along(cot[:, :, :1, :], "brick", -1)
    cot1 = jnp.concatenate([cot[:, :, 1:, :], upper], axis=2)
    wide, tall = prepare(cot.reshape(cells, out_width), cot1.reshape(cells, out_width), dims)
    bias = b_first.reshape(1, width)
    offsets = w_conv.reshape(27, width, out_width)

    grid, kernel_term = forward(recv, w_first, bias, tall, cap, vox_count)
    w_term, b_term = backward(recv, w_first, bias, wide, offsets, cap, vox_count, scale)
    flat = jnp.concatenate(
        [kernel_term.reshape(-1, LANES), w_term.astype(BF16).reshape(-1, LANES), b_term.astype(BF16).reshape(-1, LANES)], axis=0
    )
    count = flat.shape[0]
    unit = 8 * 2 * devices
    flat = jnp.pad(flat, ((0, -count % unit), (0, 0)))
    total = summed(flat).astype(F32)
    n_conv = kernel_term.size // LANES
    n_first = w_term.size // LANES
    conv_grad = total[:n_conv].reshape(w_conv.shape) * scale
    w_first_grad = total[n_conv : n_conv + n_first].reshape(width, width)
    b_first_grad = total[n_conv + n_first : count].reshape(width)

    partial, edge = convolve(grid, offsets, dims)
    below = passed_along(edge, "brick", 1).reshape(half_x, half_y, 1, out_width)
    partial = partial.reshape(half_x, half_y, half_z, out_width)
    volume_out = jnp.concatenate([partial[:, :, :1] + below, partial[:, :, 1:]], axis=2).astype(BF16)
    return (volume_out[None], conv_grad, w_first_grad, b_first_grad)


def solution(mesh):
    return jax.shard_map(
        shards,
        mesh=mesh,
        in_specs=(
            P(("dom", "brick"), None),
            P(("dom", "brick"), None),
            P(("dom", "brick")),
            P(),
            P(),
            P(),
            P("dom", None, None, "brick", None),
        ),
        out_specs=(P("dom", None, None, "brick", None), P(), P(), P()),
        check_vma=False,
    )
```

```python
import functools
import math

import jax
import jax.numpy as jnp
from jax import lax
from jax.experimental import pallas as pl
from jax.experimental.pallas import tpu as pltpu
from jax.sharding import PartitionSpec as P

BF16 = jnp.bfloat16
F32 = jnp.float32
LANES = 128
PAD = 16
VMEM = pl.BlockSpec(memory_space=pltpu.VMEM)
BIG = 48 * 2**20
SMALL = 24 * 2**20
ANY = pl.BlockSpec(memory_space=pl.ANY)


def lasting(microseconds):
    return pl.CostEstimate(
        flops=int(microseconds * 1.1e9), bytes_accessed=int(microseconds * 3.5e6), transcendentals=0
    )


def dot(a, b):
    return jnp.dot(a, b, preferred_element_type=F32)


def dot_nt(a, b):
    return lax.dot_general(a, b, (((1,), (1,)), ((), ())), preferred_element_type=F32)


def dot_tn(a, b):
    return lax.dot_general(a, b, (((0,), (0,)), ((), ())), preferred_element_type=F32)


def shifts_of(parity):
    return [s for s in range(8) if s & ~parity == 0]


def offset_of(parity, shift):
    index = 0
    for bit in (4, 2, 1):
        index = 3 * index + (1 if not parity & bit else 0 if shift & bit else 2)
    return index


def pack_kernel(group, cap, dims, half_ref, owner_ref, voxel_ref, feat_ref, out_ref, slot_ref, table_ref):
    rows = feat_ref.shape[0]
    devices = table_ref.shape[0] // 2
    half_x, half_y, half_z = dims
    cells = half_x * half_y * half_z
    first_device = half_ref[0] * devices
    step = 2 * LANES

    @pl.when(pl.program_id(0) == 0)
    def _():
        before = lax.broadcasted_iota(jnp.int32, (step, step), 0) < lax.broadcasted_iota(
            jnp.int32, (step, step), 1
        )
        before = before.astype(F32).astype(BF16)
        device = lax.broadcasted_iota(jnp.int32, (devices, step), 0)
        place = lax.broadcasted_iota(jnp.int32, (LANES, step), 0).astype(F32)
        seen = jnp.zeros((devices, 1), F32)
        table = jnp.zeros((2 * devices, LANES), F32)
        for start in range(0, rows, step):
            here = (device == owner_ref[:, start : start + step] - first_device).astype(F32)
            rank = here * (dot(here.astype(BF16), before) + seen + 1.0)
            slot = jnp.sum(rank + here * (device * cap).astype(F32), axis=0, keepdims=True) - 1.0
            slot_ref[:, start : start + step] = slot.astype(jnp.int32)
            seen = seen + jnp.sum(here, axis=1, keepdims=True)
            voxel = voxel_ref[:, start : start + step]
            z, line = voxel % (2 * half_z), voxel // (2 * half_z)
            y, x = line % (2 * half_y), line // (2 * half_y)
            parity = (x % 2) * 4 + (y % 2) * 2 + z % 2
            code = parity * cells + ((x // 2) * half_y + y // 2) * half_z + z // 2
            high, low = (code >> 7) + 1, code & 127
            values = jnp.concatenate([here * high.astype(F32), here * low.astype(F32)], axis=0)
            ranked = jnp.where(place == jnp.sum(rank, axis=0, keepdims=True) - 1.0, 1.0, 0.0)
            table = table + dot_nt(values.astype(BF16), ranked.astype(BF16))
        table_ref[...] = table

    first = pl.program_id(0) * group
    place = lax.broadcasted_iota(jnp.int32, (group * cap, rows), 0) + first * cap
    chosen = jnp.where(place == slot_ref[...], 1.0, 0.0).astype(BF16)
    packed = dot(chosen, feat_ref[...]).astype(BF16)
    for g in range(group):
        out_ref[g, :cap, :] = packed[g * cap : (g + 1) * cap]
        high = table_ref[pl.ds(first + g, 1), :]
        low = table_ref[pl.ds(devices + first + g, 1), :]
        both = jnp.concatenate([high, low], axis=1)
        out_ref[g, cap:, :] = jnp.broadcast_to(both, (PAD, 2 * LANES)).astype(BF16)


def pack(half, owner, voxel, features, cap, devices, dims):
    rows, width = features.shape
    group = max(1, 512 // cap)
    return pl.pallas_call(
        functools.partial(pack_kernel, group, cap, dims),
        out_shape=jax.ShapeDtypeStruct((devices, cap + PAD, width), BF16),
        grid_spec=pltpu.PrefetchScalarGridSpec(
            num_scalar_prefetch=1,
            grid=(devices // group,),
            in_specs=[VMEM] * 3,
            out_specs=pl.BlockSpec((group, cap + PAD, width), lambda i, half: (i, 0, 0)),
            scratch_shapes=[pltpu.VMEM((1, rows), jnp.int32), pltpu.VMEM((2 * devices, LANES), F32)],
        ),
        compiler_params=pltpu.CompilerParams(vmem_limit_bytes=SMALL),
        cost_estimate=lasting(4),
        name="pack",
    )(half, owner, voxel, features)


def lay_out(cot_ref, above_ref, dims, wide, tall):
    half_x, half_y, half_z = dims
    cells = half_x * half_y * half_z
    width = cot_ref.shape[1]
    same = cot_ref[...].astype(F32)
    above = jnp.broadcast_to(above_ref[...].astype(F32)[:, None, :], (cells // half_z, half_z, width))
    highest = lax.broadcasted_iota(jnp.int32, (cells, width), 0) % half_z == half_z - 1
    ahead = jnp.where(highest, above.reshape(cells, width), pltpu.roll(same, cells - 1, 0))
    for shift in range(8):
        values = ahead if shift & 1 else same
        if shift & 4:
            gap = half_y * half_z
            values = jnp.concatenate([values[gap:], jnp.zeros((gap, width), F32)], axis=0)
        if shift & 2:
            values = values.reshape(half_x, half_y * half_z, width)
            gone = jnp.zeros((half_x, half_z, width), F32)
            values = jnp.concatenate([values[:, half_z:], gone], axis=1).reshape(cells, width)
        wide[:, shift * width : (shift + 1) * width] = values.astype(BF16)
        tall[shift * width : (shift + 1) * width, :] = values.T.astype(BF16)


def codes_of(recv, cap, vox_count):
    parts = recv[:, cap, :].astype(jnp.int32)
    high, low = parts[:, :cap], parts[:, LANES : LANES + cap]
    return jnp.where(high > 0, (high - 1) * 128 + low, vox_count).reshape(-1)


def put_rows(ref, start, values):
    count = values.shape[0]
    ref[pl.ds(2 * start, count, stride=2), :] = values[:, :LANES]
    ref[pl.ds(2 * start + 1, count, stride=2), :] = values[:, LANES:]


def get_rows(ref, start, count):
    low = ref[pl.ds(2 * start, count, stride=2), :]
    high = ref[pl.ds(2 * start + 1, count, stride=2), :]
    return low, high


UNROLL = 16
CHUNK = 512


def pairs_of(ref):
    return ref.reshape(ref.shape[0] // 2, 2, LANES)


def add_products(block, conv_ref, parity, dims, same, next_):
    half_x, half_y, half_z = dims
    plane = half_y * half_z
    width = conv_ref.shape[2]
    shifts = shifts_of(parity)
    right = jnp.concatenate([conv_ref[offset_of(parity, s)] for s in shifts], axis=1)
    product = dot(block, right)
    for at, s in enumerate(shifts):
        part = product[:, at * width : (at + 1) * width].reshape(half_x, plane, width)
        dx = 1 if s & 4 else 0
        dy = half_z if s & 2 else 0
        total = next_ if s & 1 else same
        total[dx:, dy:, :] += part[: half_x - dx, : plane - dy, :]


def shifted_along_z(same, next_, dims):
    half_x, half_y, half_z = dims
    cells = half_x * half_y * half_z
    width = same.shape[2]
    after = next_[...].reshape(cells, width)
    lowest = lax.broadcasted_iota(jnp.int32, (cells, width), 0) % half_z == 0
    total = same[...].reshape(cells, width) + jnp.where(lowest, 0.0, pltpu.roll(after, 1, 0))
    return total, after.reshape(cells // half_z, half_z, width)[:, half_z - 1, :]


def slab_kernel(cap, scale, far, dims, *refs):
    codes, recv_ref, w_ref, b_ref, cot_ref, above_ref, conv_hbm = refs[:7]
    if far:
        terms_hbm, wterm_ref, bterm_ref, lent_ref, flat_ref = refs[7:12]
        sums, rows, slopes, tall, wide, conv, terms, sems, wgrad, bgrad, same, next_ = refs[12:]
    else:
        grid_hbm, terms_hbm, wgrad, bgrad, sums, rows, slopes, tall, wide, conv, terms, sems, stage = refs[7:]
    sources, _, width = recv_ref.shape
    half_x, half_y, half_z = dims
    cells = half_x * half_y * half_z
    vox_count = 8 * cells
    out_width = conv.shape[2]
    count = sources * cap
    loads = [pltpu.make_async_copy(conv_hbm, conv, sems.at[0])]
    if far:
        loads.append(pltpu.make_async_copy(terms_hbm, terms, sems.at[3]))
    for load in loads:
        load.start()
    lay_out(cot_ref, above_ref, dims, wide, tall)

    def clear(i, _):
        sums[pl.ds(pl.multiple_of(i * 1024, 1024), 1024), :] = jnp.zeros((1024, LANES), F32)
        return 0

    lax.fori_loop(0, vox_count // 512, clear, 0)
    step = CHUNK // cap

    def layer(i, _):
        feats = recv_ref[pl.ds(i * step, step), :cap, :].reshape(CHUNK, width)
        pre = dot(feats, w_ref[...]) + b_ref[...]
        sig = jax.nn.sigmoid(pre)
        put_rows(rows, i * CHUNK, (pre * sig).astype(BF16).astype(F32))
        slopes[pl.ds(i * CHUNK, CHUNK), :] = sig * (1.0 + pre * (1.0 - sig))
        return 0

    lax.fori_loop(0, count // CHUNK, layer, 0)
    sum_rows, new_rows = pairs_of(sums), pairs_of(rows)

    def add(i, _):
        for u in range(0, UNROLL, 2):
            at = i * UNROLL + u
            a, b = codes[at], codes[at + 1]
            old_a, old_b = sum_rows[a], sum_rows[b]
            new_a = old_a + new_rows[at]
            new_b = jnp.where(a == b, new_a, old_b) + new_rows[at + 1]
            sum_rows[a] = new_a
            sum_rows[b] = new_b
        return 0

    lax.fori_loop(0, count // UNROLL, add, 0)
    for load in loads:
        load.wait()
    if far:
        same[...] = jnp.zeros_like(same)
        next_[...] = jnp.zeros_like(next_)
    stores = []
    for parity in range(8):
        low, high = get_rows(sums, parity * cells, cells)
        block = jnp.concatenate([low.astype(BF16), high.astype(BF16)], axis=1)
        if not far:
            if parity >= 2:
                stores[parity - 2].wait()
            stage[parity % 2] = block
            stores.append(pltpu.make_async_copy(stage.at[parity % 2], grid_hbm.at[parity], sems.at[4 + parity % 2]))
            stores[parity].start()
        shifts = shifts_of(parity)
        left = jnp.concatenate([tall[s * out_width : (s + 1) * out_width, :] for s in shifts], axis=0)
        grads = dot(left, block)
        for at, s in enumerate(shifts):
            first = offset_of(parity, s) * width
            grad = grads[at * out_width : (at + 1) * out_width].T
            if far:
                flat_ref[first : first + width, :] = (grad + terms[first : first + width, :]).astype(BF16)
            else:
                terms[first : first + width, :] = grad
        if far:
            add_products(block, conv, parity, dims, same, next_)
        left = jnp.concatenate([wide[:, s * out_width : (s + 1) * out_width] for s in shifts], axis=1)
        right = jnp.concatenate([conv[offset_of(parity, s)] for s in shifts], axis=1)
        put_rows(sums, parity * cells, (dot_nt(left, right) * scale).astype(BF16).astype(F32))
    sums[2 * vox_count :, :] = jnp.zeros((16, LANES), F32)
    if not far:
        stores = stores[-2:] + [pltpu.make_async_copy(terms, terms_hbm, sems.at[3])]
        stores[-1].start()
    else:
        total, edge = shifted_along_z(same, next_, dims)
        lent_ref[:cells, :] = total.astype(BF16)
        lent_ref[cells:, :] = edge.astype(BF16)

    def take(i, _):
        for u in range(UNROLL):
            at = i * UNROLL + u
            new_rows[at] = sum_rows[codes[at]]
        return 0

    lax.fori_loop(0, count // UNROLL, take, 0)
    wgrad[...] = wterm_ref[...] if far else jnp.zeros_like(wgrad)
    bgrad[...] = bterm_ref[...] if far else jnp.zeros_like(bgrad)

    def layer_back(i, _):
        feats = recv_ref[pl.ds(i * step, step), :cap, :].reshape(CHUNK, width)
        low, high = get_rows(rows, i * CHUNK, CHUNK)
        pre_grad = (jnp.concatenate([low, high], axis=1) * slopes[pl.ds(i * CHUNK, CHUNK), :]).astype(BF16)
        wgrad[...] += dot_tn(feats, pre_grad)
        bgrad[...] += jnp.sum(pre_grad.astype(F32), axis=0, keepdims=True)
        return 0

    lax.fori_loop(0, count // CHUNK, layer_back, 0)
    if far:
        first = 27 * width
        flat_ref[first : first + width, :] = wgrad[:, :LANES].astype(BF16)
        flat_ref[first + width : first + 2 * width, :] = wgrad[:, LANES:].astype(BF16)
        first += 2 * width
        bias = bgrad[...]
        row = lax.broadcasted_iota(jnp.int32, (PAD, LANES), 0)
        bias = jnp.where(row == 0, bias[:, :LANES], jnp.where(row == 1, bias[:, LANES:], 0.0))
        flat_ref[first : first + PAD, :] = bias.astype(BF16)
        first += PAD
        flat_ref[first:, :] = jnp.zeros((flat_ref.shape[0] - first, LANES), BF16)
    for store in stores:
        store.wait()


def slab(codes, recv, w_first, b_first, cot, above, w_conv, cap, scale, dims, earlier=None, length=None):
    sources, _, width = recv.shape
    half_x, half_y, half_z = dims
    cells = half_x * half_y * half_z
    out_width = w_conv.shape[2]
    far = earlier is not None
    n_conv = 27 * width
    count = sources * cap
    operands = (recv, w_first, b_first, cot, above, w_conv)
    in_specs = [VMEM] * 5 + [ANY]
    scratch = [
        pltpu.VMEM((2 * 8 * cells + 16, LANES), F32),
        pltpu.VMEM((2 * count, LANES), F32),
        pltpu.VMEM((count, width), F32),
        pltpu.VMEM((8 * out_width, cells), BF16),
        pltpu.VMEM((cells, 8 * out_width), BF16),
        pltpu.VMEM(w_conv.shape, BF16),
        pltpu.VMEM((n_conv, LANES), F32),
        pltpu.SemaphoreType.DMA((6,)),
    ]
    if far:
        operands += tuple(earlier)
        in_specs += [ANY, VMEM, VMEM]
        out_shape = (
            jax.ShapeDtypeStruct((cells + cells // half_z, out_width), BF16),
            jax.ShapeDtypeStruct((length, LANES), BF16),
        )
        out_specs = (VMEM, VMEM)
        scratch += [pltpu.VMEM((width, width), F32), pltpu.VMEM((1, width), F32)]
        scratch += [pltpu.VMEM((half_x, half_y * half_z, out_width), F32)] * 2
    else:
        out_shape = (
            jax.ShapeDtypeStruct((8, cells, width), BF16),
            jax.ShapeDtypeStruct((n_conv, LANES), F32),
            jax.ShapeDtypeStruct((width, width), F32),
            jax.ShapeDtypeStruct((1, width), F32),
        )
        out_specs = (ANY, ANY, VMEM, VMEM)
        scratch += [pltpu.VMEM((2, cells, width), BF16)]
    return pl.pallas_call(
        functools.partial(slab_kernel, cap, scale, far, dims),
        out_shape=out_shape,
        grid_spec=pltpu.PrefetchScalarGridSpec(
            num_scalar_prefetch=1, grid=(1,), in_specs=in_specs, out_specs=out_specs, scratch_shapes=scratch
        ),
        compiler_params=pltpu.CompilerParams(vmem_limit_bytes=BIG),
        cost_estimate=lasting(28),
        name="slab_far" if far else "slab_near",
    )(codes, *operands)


def convolve_kernel(dims, grid_ref, conv_ref, out_ref, edge_ref, same, next_):
    same[...] = jnp.zeros_like(same)
    next_[...] = jnp.zeros_like(next_)
    for parity in range(8):
        add_products(grid_ref[parity], conv_ref, parity, dims, same, next_)
    out_ref[...], edge_ref[...] = shifted_along_z(same, next_, dims)


def convolve(grid, w_conv, dims):
    half_x, half_y, half_z = dims
    cells = half_x * half_y * half_z
    width = w_conv.shape[2]
    return pl.pallas_call(
        functools.partial(convolve_kernel, dims),
        out_shape=(
            jax.ShapeDtypeStruct((cells, width), F32),
            jax.ShapeDtypeStruct((cells // half_z, width), F32),
        ),
        in_specs=[VMEM] * 2,
        out_specs=(VMEM, VMEM),
        scratch_shapes=[pltpu.VMEM((half_x, half_y * half_z, width), F32)] * 2,
        compiler_params=pltpu.CompilerParams(vmem_limit_bytes=BIG),
        cost_estimate=lasting(9),
        name="convolve",
    )(grid, w_conv)


def finish_kernel(scale, bit_ref, mine_ref, theirs_ref, conv_ref, w_ref, b_ref):
    half = mine_ref.shape[0]
    width = w_ref.shape[0]
    n_conv = conv_ref.shape[0]

    def write(low_ref, high_ref):
        conv_ref[:half, :] = low_ref[...].astype(F32) * scale
        rest = n_conv - half
        conv_ref[half:, :] = high_ref[:rest, :].astype(F32) * scale
        w_ref[:, :LANES] = high_ref[rest : rest + width, :].astype(F32)
        w_ref[:, LANES:] = high_ref[rest + width : rest + 2 * width, :].astype(F32)
        rest += 2 * width
        bias = high_ref[rest : rest + PAD, :].astype(F32)
        b_ref[...] = jnp.concatenate([bias[0:1], bias[1:2]], axis=1)

    @pl.when(bit_ref[0] == 0)
    def _():
        write(mine_ref, theirs_ref)

    @pl.when(bit_ref[0] == 1)
    def _():
        write(theirs_ref, mine_ref)


def finish(bit, mine, theirs, n_conv, width, scale):
    return pl.pallas_call(
        functools.partial(finish_kernel, scale),
        out_shape=(
            jax.ShapeDtypeStruct((n_conv, LANES), F32),
            jax.ShapeDtypeStruct((width, width), F32),
            jax.ShapeDtypeStruct((1, width), F32),
        ),
        grid_spec=pltpu.PrefetchScalarGridSpec(
            num_scalar_prefetch=1, grid=(1,), in_specs=[VMEM] * 2, out_specs=(VMEM,) * 3
        ),
        compiler_params=pltpu.CompilerParams(vmem_limit_bytes=BIG),
        cost_estimate=lasting(4),
        name="finish",
    )(bit, mine, theirs)


AXES = ("half", "dom", "brick")


def passed_along(array, axis, by):
    size = lax.axis_size(axis)
    pairs = [(i, i + by) for i in range(size) if 0 <= i + by < size]
    return lax.ppermute(array, axis, pairs)


def crossed(array):
    return lax.ppermute(array, "half", [(0, 1), (1, 0)])


def exchange(array, mask):
    return lax.ppermute(array, AXES, [(i, i ^ mask) for i in range(lax.axis_size(AXES))])


def bit_groups():
    bits = lax.axis_size(AXES).bit_length() - 1
    return [(0, 1)] + [(at, min(2, bits - at)) for at in range(1, bits, 2)]


def reduced(part, me, first, count):
    blocks = part.reshape(1 << count, -1, LANES)
    mine = (me >> first) & ((1 << count) - 1)
    arrived = [
        exchange(lax.dynamic_index_in_dim(blocks, mine ^ m, 0, keepdims=False), m << first)
        for m in range(1, 1 << count)
    ]
    total = lax.dynamic_index_in_dim(blocks, mine, 0, keepdims=False).astype(F32)
    for block in arrived:
        total = total + block.astype(F32)
    return total.astype(BF16)


def gathered(part, me, first, count):
    blocks = [part] + [exchange(part, m << first) for m in range(1, 1 << count)]
    for bit in range(count):
        swap = (me >> (first + bit)) & 1 == 1
        blocks = [jnp.where(swap, blocks[i ^ (1 << bit)], blocks[i]) for i in range(1 << count)]
    return jnp.concatenate(blocks, axis=0)


def shards(features, elem_owner, elem_voxel, w_first, b_first, w_conv, cotangent):
    n_brick = lax.axis_size("brick")
    devices = lax.axis_size(AXES)
    near = devices // 2
    me = lax.axis_index(AXES)
    rows, width = features.shape
    cap = 2 * rows // devices
    dims = cotangent.shape[1:4]
    half_x, half_y, half_z = dims
    cells = half_x * half_y * half_z
    vox_count = 8 * cells
    out_width = cotangent.shape[4]
    scale = 1.0 / math.sqrt(devices * cells)
    bias = b_first.reshape(1, width)
    offsets = w_conv.reshape(27, width, out_width)

    cot = cotangent.reshape(cells, out_width)
    plane = cotangent[0, :, :, 0, :].reshape(-1, out_width)
    above = passed_along(plane, "brick", -1)
    slabs = [(i, i - 1) for i in range(devices) if i % n_brick]
    far_above = lax.ppermute(plane, AXES, [(i, j ^ near) for i, j in slabs])
    far_cot = crossed(cot)

    half = lax.axis_index("half").reshape(1)
    owner, voxel = elem_owner.reshape(1, rows), elem_voxel.reshape(1, rows)

    def swapped(packed):
        return lax.all_to_all(packed, ("dom", "brick"), split_axis=0, concat_axis=0, tiled=True)

    near_recv = swapped(pack(half, owner, voxel, features, cap, near, dims))
    far_packed = pack(1 - half, owner, voxel, features, cap, near, dims)
    far_recv = swapped(far_packed)

    n_conv = 27 * width
    length = -(-(n_conv + 2 * width + PAD) // (8 * devices)) * (8 * devices)
    near_codes = codes_of(near_recv, cap, vox_count)
    near_grid, *terms = slab(near_codes, near_recv, w_first, bias, cot, above, offsets, cap, scale, dims)
    far_codes = codes_of(far_recv, cap, vox_count)
    lent, part = slab(
        far_codes, far_recv, w_first, bias, far_cot, far_above, offsets, cap, scale, dims, terms, length
    )
    lent = crossed(lent)

    groups = bit_groups()
    for step, (first, count) in enumerate(groups):
        part = reduced(part, me, first, count)
        if step == 1:
            part, lent = lax.optimization_barrier((part, lent))
    for first, count in reversed(groups[1:]):
        part = gathered(part, me, first, count)
    conv_grad, w_first_grad, b_first_grad = finish(
        (me & 1).reshape(1), part, exchange(part, 1), n_conv, width, scale
    )

    lent = lent.astype(F32)
    near_out, near_edge = convolve(near_grid, offsets, dims)
    below = passed_along(near_edge + lent[cells:], "brick", 1).reshape(half_x, half_y, 1, out_width)
    whole = (near_out + lent[:cells]).reshape(half_x, half_y, half_z, out_width)
    volume_out = jnp.concatenate([whole[:, :, :1] + below, whole[:, :, 1:]], axis=2).astype(BF16)
    return (
        volume_out[None],
        conv_grad.reshape(w_conv.shape),
        w_first_grad,
        b_first_grad.reshape(width),
    )


def solution(mesh):
    n_dom, n_brick = mesh.devices.shape
    halves = jax.sharding.Mesh(mesh.devices.reshape(2, n_dom // 2, n_brick), AXES)
    bricks = P(("half", "dom"), None, None, "brick", None)
    return jax.shard_map(
        shards,
        mesh=halves,
        in_specs=(P(AXES, None), P(AXES, None), P(AXES), P(), P(), P(), bricks),
        out_specs=(bricks, P(), P(), P()),
        check_vma=False,
    )
```

```python
import functools
import math

import jax
import jax.numpy as jnp
from jax import lax
from jax.experimental import pallas as pl
from jax.experimental.pallas import tpu as pltpu
from jax.sharding import PartitionSpec as P

BF16 = jnp.bfloat16
F32 = jnp.float32
LANES = 128
PAD = 16
VMEM = pl.BlockSpec(memory_space=pltpu.VMEM)
BIG = 56 * 2**20
SMALL = 24 * 2**20
ANY = pl.BlockSpec(memory_space=pl.ANY)


def lasting(microseconds):
    return pl.CostEstimate(
        flops=int(microseconds * 1.1e9), bytes_accessed=int(microseconds * 3.5e6), transcendentals=0
    )


def dot(a, b):
    return jnp.dot(a, b, preferred_element_type=F32)


def dot_nt(a, b):
    return lax.dot_general(a, b, (((1,), (1,)), ((), ())), preferred_element_type=F32)


def dot_tn(a, b):
    return lax.dot_general(a, b, (((0,), (0,)), ((), ())), preferred_element_type=F32)


def shifts_of(parity):
    return [s for s in range(8) if s & ~parity == 0]


def offset_of(parity, shift):
    index = 0
    for bit in (4, 2, 1):
        index = 3 * index + (1 if not parity & bit else 0 if shift & bit else 2)
    return index


def pack_kernel(group, cap, dims, half_ref, owner_ref, voxel_ref, feat_ref, out_ref, slot_ref, table_ref):
    rows = feat_ref.shape[0]
    devices = table_ref.shape[0] // 2
    half_x, half_y, half_z = dims
    cells = half_x * half_y * half_z
    first_device = half_ref[0] * devices
    step = 2 * LANES

    @pl.when(pl.program_id(0) == 0)
    def _():
        before = lax.broadcasted_iota(jnp.int32, (step, step), 0) < lax.broadcasted_iota(
            jnp.int32, (step, step), 1
        )
        before = before.astype(F32).astype(BF16)
        device = lax.broadcasted_iota(jnp.int32, (devices, step), 0)
        place = lax.broadcasted_iota(jnp.int32, (LANES, step), 0).astype(F32)
        seen = jnp.zeros((devices, 1), F32)
        table = jnp.zeros((2 * devices, LANES), F32)
        for start in range(0, rows, step):
            here = (device == owner_ref[:, start : start + step] - first_device).astype(F32)
            rank = here * (dot(here.astype(BF16), before) + seen + 1.0)
            slot = jnp.sum(rank + here * (device * cap).astype(F32), axis=0, keepdims=True) - 1.0
            slot_ref[:, start : start + step] = slot.astype(jnp.int32)
            seen = seen + jnp.sum(here, axis=1, keepdims=True)
            voxel = voxel_ref[:, start : start + step]
            z, line = voxel % (2 * half_z), voxel // (2 * half_z)
            y, x = line % (2 * half_y), line // (2 * half_y)
            parity = (x % 2) * 4 + (y % 2) * 2 + z % 2
            code = parity * cells + ((x // 2) * half_y + y // 2) * half_z + z // 2
            high, low = (code >> 7) + 1, code & 127
            values = jnp.concatenate([here * high.astype(F32), here * low.astype(F32)], axis=0)
            ranked = jnp.where(place == jnp.sum(rank, axis=0, keepdims=True) - 1.0, 1.0, 0.0)
            table = table + dot_nt(values.astype(BF16), ranked.astype(BF16))
        table_ref[...] = table

    first = pl.program_id(0) * group
    place = lax.broadcasted_iota(jnp.int32, (group * cap, rows), 0) + first * cap
    chosen = jnp.where(place == slot_ref[...], 1.0, 0.0).astype(BF16)
    packed = dot(chosen, feat_ref[...]).astype(BF16)
    for g in range(group):
        out_ref[g, :cap, :] = packed[g * cap : (g + 1) * cap]
        high = table_ref[pl.ds(first + g, 1), :]
        low = table_ref[pl.ds(devices + first + g, 1), :]
        both = jnp.concatenate([high, low], axis=1)
        out_ref[g, cap:, :] = jnp.broadcast_to(both, (PAD, 2 * LANES)).astype(BF16)


def pack(half, owner, voxel, features, cap, devices, dims):
    rows, width = features.shape
    group = max(1, 512 // cap)
    return pl.pallas_call(
        functools.partial(pack_kernel, group, cap, dims),
        out_shape=jax.ShapeDtypeStruct((devices, cap + PAD, width), BF16),
        grid_spec=pltpu.PrefetchScalarGridSpec(
            num_scalar_prefetch=1,
            grid=(devices // group,),
            in_specs=[VMEM] * 3,
            out_specs=pl.BlockSpec((group, cap + PAD, width), lambda i, half: (i, 0, 0)),
            scratch_shapes=[pltpu.VMEM((1, rows), jnp.int32), pltpu.VMEM((2 * devices, LANES), F32)],
        ),
        compiler_params=pltpu.CompilerParams(vmem_limit_bytes=BIG),
        cost_estimate=lasting(4),
        name="pack",
    )(half, owner, voxel, features)


def lay_out(cot_ref, dims, wide, tall):
    half_x, half_y, half_z = dims
    cells = half_x * half_y * half_z
    width = cot_ref.shape[1]
    same = cot_ref[:cells, :].astype(F32)
    above = jnp.broadcast_to(cot_ref[cells:, :].astype(F32)[:, None, :], (cells // half_z, half_z, width))
    highest = lax.broadcasted_iota(jnp.int32, (cells, width), 0) % half_z == half_z - 1
    ahead = jnp.where(highest, above.reshape(cells, width), pltpu.roll(same, cells - 1, 0))
    for shift in range(8):
        values = ahead if shift & 1 else same
        if shift & 4:
            gap = half_y * half_z
            values = jnp.concatenate([values[gap:], jnp.zeros((gap, width), F32)], axis=0)
        if shift & 2:
            values = values.reshape(half_x, half_y * half_z, width)
            gone = jnp.zeros((half_x, half_z, width), F32)
            values = jnp.concatenate([values[:, half_z:], gone], axis=1).reshape(cells, width)
        if wide is not None:
            wide[:, shift * width : (shift + 1) * width] = values.astype(BF16)
        if tall is not None:
            tall[shift * width : (shift + 1) * width, :] = values.T.astype(BF16)


def codes_of(recv, cap, vox_count):
    parts = recv[:, cap, :].astype(jnp.int32)
    high, low = parts[:, :cap], parts[:, LANES : LANES + cap]
    return jnp.where(high > 0, (high - 1) * 128 + low, vox_count).reshape(-1)


def put_rows(ref, start, values):
    count = values.shape[0]
    ref[pl.ds(2 * start, count, stride=2), :] = values[:, :LANES]
    ref[pl.ds(2 * start + 1, count, stride=2), :] = values[:, LANES:]


def get_rows(ref, start, count):
    low = ref[pl.ds(2 * start, count, stride=2), :]
    high = ref[pl.ds(2 * start + 1, count, stride=2), :]
    return low, high


UNROLL = 16
CHUNK = 512


def pairs_of(ref):
    return ref.reshape(ref.shape[0] // 2, 2, LANES)


def add_products(block, conv_ref, parity, dims, same, next_):
    half_x, half_y, half_z = dims
    plane = half_y * half_z
    width = conv_ref.shape[2]
    shifts = shifts_of(parity)
    right = jnp.concatenate([conv_ref[offset_of(parity, s)] for s in shifts], axis=1)
    product = dot(block, right)
    for at, s in enumerate(shifts):
        part = product[:, at * width : (at + 1) * width].reshape(half_x, plane, width)
        dx = 1 if s & 4 else 0
        dy = half_z if s & 2 else 0
        total = next_ if s & 1 else same
        total[dx:, dy:, :] += part[: half_x - dx, : plane - dy, :]


def shifted_along_z(same, next_, dims):
    half_x, half_y, half_z = dims
    cells = half_x * half_y * half_z
    width = same.shape[2]
    after = next_[...].reshape(cells, width)
    lowest = lax.broadcasted_iota(jnp.int32, (cells, width), 0) % half_z == 0
    total = same[...].reshape(cells, width) + jnp.where(lowest, 0.0, pltpu.roll(after, 1, 0))
    return total, after.reshape(cells // half_z, half_z, width)[:, half_z - 1, :]


def slab_kernel(cap, scale, dims, kind, *refs):
    ahead, back, far = kind != "far_back", kind != "far_ahead", kind != "near"
    bit, codes, recv_ref, w_ref, b_ref, cot_ref, conv_hbm = refs[:7]
    wide = tall = slopes = None
    if kind == "near":
        out_ref, edge_ref, terms_hbm, wgrad, bgrad, sums, rows, conv, sems, slopes, wide, tall, terms, same, next_ = refs[7:]
    elif kind == "far_ahead":
        terms_hbm, lent_ref, rest_ref, keep_hbm, send_hbm, sums, rows, conv, sems, tall, terms, flat, same, next_ = refs[7:]
    else:
        wterm_ref, bterm_ref, first_ref, sums, rows, conv, sems, slopes, wide, wgrad, bgrad = refs[7:]
    sources, _, width = recv_ref.shape
    half_x, half_y, half_z = dims
    cells = half_x * half_y * half_z
    vox_count = 8 * cells
    out_width = conv.shape[2]
    count = sources * cap
    loads = [pltpu.make_async_copy(conv_hbm, conv, sems.at[0])]
    if kind == "far_ahead":
        loads.append(pltpu.make_async_copy(terms_hbm, terms, sems.at[1]))
    for load in loads:
        load.start()
    lay_out(cot_ref, dims, wide, tall)
    step = CHUNK // cap
    sum_rows, new_rows = pairs_of(sums), pairs_of(rows)

    def layer(i, _):
        feats = recv_ref[pl.ds(i * step, step), :cap, :].reshape(CHUNK, width)
        pre = dot(feats, w_ref[...]) + b_ref[...]
        sig = jax.nn.sigmoid(pre)
        if ahead:
            put_rows(rows, i * CHUNK, (pre * sig).astype(BF16).astype(F32))
        if back:
            slopes[pl.ds(i * CHUNK, CHUNK), :] = sig * (1.0 + pre * (1.0 - sig))
        return 0

    lax.fori_loop(0, count // CHUNK, layer, 0)
    if ahead:

        def clear(i, _):
            sums[pl.ds(pl.multiple_of(i * 1024, 1024), 1024), :] = jnp.zeros((1024, LANES), F32)
            return 0

        lax.fori_loop(0, vox_count // 512, clear, 0)

        def add(i, _):
            for u in range(0, UNROLL, 2):
                at = i * UNROLL + u
                a, b = codes[at], codes[at + 1]
                old_a, old_b = sum_rows[a], sum_rows[b]
                new_a = old_a + new_rows[at]
                new_b = jnp.where(a == b, new_a, old_b) + new_rows[at + 1]
                sum_rows[a] = new_a
                sum_rows[b] = new_b
            return 0

        lax.fori_loop(0, count // UNROLL, add, 0)
    for load in loads:
        load.wait()
    if ahead:
        same[...] = jnp.zeros_like(same)
        next_[...] = jnp.zeros_like(next_)
    stores = []
    for parity in range(8):
        shifts = shifts_of(parity)
        if ahead:
            low, high = get_rows(sums, parity * cells, cells)
            block = jnp.concatenate([low.astype(BF16), high.astype(BF16)], axis=1)
            left = jnp.concatenate([tall[s * out_width : (s + 1) * out_width, :] for s in shifts], axis=0)
            grads = dot(left, block)
            for at, s in enumerate(shifts):
                first = offset_of(parity, s) * width
                grad = grads[at * out_width : (at + 1) * out_width].T
                if far:
                    flat[first : first + width, :] = (grad + terms[first : first + width, :]).astype(BF16)
                else:
                    terms[first : first + width, :] = grad
            add_products(block, conv, parity, dims, same, next_)
        if back:
            left = jnp.concatenate([wide[:, s * out_width : (s + 1) * out_width] for s in shifts], axis=1)
            right = jnp.concatenate([conv[offset_of(parity, s)] for s in shifts], axis=1)
            put_rows(sums, parity * cells, (dot_nt(left, right) * scale).astype(BF16).astype(F32))
    if kind == "near":
        out_ref[...], edge_ref[...] = shifted_along_z(same, next_, dims)
        stores.append(pltpu.make_async_copy(terms, terms_hbm, sems.at[1]))
        stores[-1].start()
    if kind == "far_ahead":
        size = flat.shape[0] // 2
        mine = pl.multiple_of(bit[0] * size, 16)
        other = pl.multiple_of((1 - bit[0]) * size, 16)
        stores = [
            pltpu.make_async_copy(flat.at[pl.ds(mine, size)], keep_hbm, sems.at[2]),
            pltpu.make_async_copy(flat.at[pl.ds(other, size)], send_hbm, sems.at[3]),
        ]
        for store in stores:
            store.start()
        total, edge = shifted_along_z(same, next_, dims)
        cut = lent_ref.shape[0]
        lent_ref[...] = total[:cut].astype(BF16)
        rest_ref[: cells - cut, :] = total[cut:].astype(BF16)
        rest_ref[cells - cut :, :] = edge.astype(BF16)
    if back:
        sums[2 * vox_count :, :] = jnp.zeros((16, LANES), F32)

        def take(i, _):
            for u in range(UNROLL):
                at = i * UNROLL + u
                new_rows[at] = sum_rows[codes[at]]
            return 0

        lax.fori_loop(0, count // UNROLL, take, 0)
        wgrad[...] = wterm_ref[...] if far else jnp.zeros_like(wgrad)
        bgrad[...] = bterm_ref[...] if far else jnp.zeros_like(bgrad)

        def layer_back(i, _):
            feats = recv_ref[pl.ds(i * step, step), :cap, :].reshape(CHUNK, width)
            low, high = get_rows(rows, i * CHUNK, CHUNK)
            pre_grad = (jnp.concatenate([low, high], axis=1) * slopes[pl.ds(i * CHUNK, CHUNK), :]).astype(BF16)
            wgrad[...] += dot_tn(feats, pre_grad)
            bgrad[...] += jnp.sum(pre_grad.astype(F32), axis=0, keepdims=True)
            return 0

        lax.fori_loop(0, count // CHUNK, layer_back, 0)
    if kind == "far_back":
        first_ref[:width, :] = wgrad[:, :LANES].astype(BF16)
        first_ref[width : 2 * width, :] = wgrad[:, LANES:].astype(BF16)
        bias = bgrad[...]
        row = lax.broadcasted_iota(jnp.int32, (PAD, LANES), 0)
        bias = jnp.where(row == 0, bias[:, :LANES], jnp.where(row == 1, bias[:, LANES:], 0.0))
        first_ref[2 * width : 2 * width + PAD, :] = bias.astype(BF16)
        rest = first_ref.shape[0] - 2 * width - PAD
        first_ref[2 * width + PAD :, :] = jnp.zeros((rest, LANES), BF16)
    for store in stores:
        store.wait()


def slab(kind, bit, codes, recv, w_first, b_first, cot, w_conv, cap, scale, dims, earlier=(), length=None):
    sources, _, width = recv.shape
    half_x, half_y, half_z = dims
    cells = half_x * half_y * half_z
    out_width = w_conv.shape[2]
    n_conv = 27 * width
    count = sources * cap
    operands = (recv, w_first, b_first, cot, w_conv) + tuple(earlier)
    in_specs = [VMEM] * 4 + [ANY]
    scratch = [
        pltpu.VMEM((2 * 8 * cells + 16, LANES), F32),
        pltpu.VMEM((2 * count, LANES), F32),
        pltpu.VMEM(w_conv.shape, BF16),
        pltpu.SemaphoreType.DMA((4,)),
    ]
    slopes = pltpu.VMEM((count, width), F32)
    wide = pltpu.VMEM((cells, 8 * out_width), BF16)
    tall = pltpu.VMEM((8 * out_width, cells), BF16)
    terms = pltpu.VMEM((n_conv, LANES), F32)
    outputs = [pltpu.VMEM((half_x, half_y * half_z, out_width), F32)] * 2
    first_layer = (jax.ShapeDtypeStruct((width, width), F32), jax.ShapeDtypeStruct((1, width), F32))
    if kind == "near":
        out_shape = (
            jax.ShapeDtypeStruct((cells, out_width), F32),
            jax.ShapeDtypeStruct((cells // half_z, out_width), F32),
            jax.ShapeDtypeStruct((n_conv, LANES), F32),
        ) + first_layer
        out_specs = (VMEM, VMEM, ANY, VMEM, VMEM)
        scratch += [slopes, wide, tall, terms] + outputs
    elif kind == "far_ahead":
        in_specs += [ANY]
        lent = (cells + cells // half_z) * 3 // 4
        out_shape = (
            jax.ShapeDtypeStruct((lent, out_width), BF16),
            jax.ShapeDtypeStruct((cells + cells // half_z - lent, out_width), BF16),
            jax.ShapeDtypeStruct((n_conv // 2, LANES), BF16),
            jax.ShapeDtypeStruct((n_conv // 2, LANES), BF16),
        )
        out_specs = (VMEM, VMEM, ANY, ANY)
        scratch += [tall, terms, pltpu.VMEM((n_conv, LANES), BF16)]
        scratch += outputs
    else:
        in_specs += [VMEM, VMEM]
        out_shape = jax.ShapeDtypeStruct((length, LANES), BF16)
        out_specs = VMEM
        scratch += [slopes, wide, pltpu.VMEM((width, width), F32), pltpu.VMEM((1, width), F32)]
    return pl.pallas_call(
        functools.partial(slab_kernel, cap, scale, dims, kind),
        out_shape=out_shape,
        grid_spec=pltpu.PrefetchScalarGridSpec(
            num_scalar_prefetch=2, grid=(1,), in_specs=in_specs, out_specs=out_specs, scratch_shapes=scratch
        ),
        compiler_params=pltpu.CompilerParams(vmem_limit_bytes=BIG),
        cost_estimate=lasting({"near": 26, "far_ahead": 20, "far_back": 11}[kind]),
        name="slab_" + kind,
    )(bit, codes, *operands)


def finish_kernel(scale, n_block, bit_ref, mine_ref, theirs_ref, conv_ref, w_ref, b_ref, first):
    width = w_ref.shape[0]
    n_conv = conv_ref.shape[0] // 8
    n_first = n_block - n_conv

    def write(refs):
        for k in range(8):
            source, at = refs[k // 4], k % 4 * n_block
            conv_ref[k * n_conv : (k + 1) * n_conv, :] = source[at : at + n_conv, :].astype(F32) * scale
            first[k * n_first : (k + 1) * n_first, :] = source[at + n_conv : at + n_block, :].astype(F32)
        w_ref[:, :LANES] = first[:width, :]
        w_ref[:, LANES:] = first[width : 2 * width, :]
        bias = first[2 * width : 2 * width + 8, :]
        b_ref[...] = jnp.concatenate([bias[0:1], bias[1:2]], axis=1)

    @pl.when(bit_ref[0] == 0)
    def _():
        write((mine_ref, theirs_ref))

    @pl.when(bit_ref[0] == 1)
    def _():
        write((theirs_ref, mine_ref))


def finish(bit, mine, theirs, n_conv, width, scale):
    n_block = mine.shape[0] // 4
    return pl.pallas_call(
        functools.partial(finish_kernel, scale, n_block),
        out_shape=(
            jax.ShapeDtypeStruct((n_conv, LANES), F32),
            jax.ShapeDtypeStruct((width, width), F32),
            jax.ShapeDtypeStruct((1, width), F32),
        ),
        grid_spec=pltpu.PrefetchScalarGridSpec(
            num_scalar_prefetch=1,
            grid=(1,),
            in_specs=[VMEM] * 2,
            out_specs=(VMEM,) * 3,
            scratch_shapes=[pltpu.VMEM((8 * n_block - n_conv, LANES), F32)],
        ),
        compiler_params=pltpu.CompilerParams(vmem_limit_bytes=SMALL),
        cost_estimate=lasting(3),
        name="finish",
    )(bit, mine, theirs)


AXES = ("half", "dom", "brick")


def passed_along(array, axis, by):
    size = lax.axis_size(axis)
    pairs = [(i, i + by) for i in range(size) if 0 <= i + by < size]
    return lax.ppermute(array, axis, pairs)


def crossed(array):
    return lax.ppermute(array, "half", [(0, 1), (1, 0)])


def exchange(array, mask):
    return lax.ppermute(array, AXES, [(i, i ^ mask) for i in range(lax.axis_size(AXES))])


def bit_groups():
    bits = lax.axis_size(AXES).bit_length() - 1
    return [(0, 1)] + [(at, min(2, bits - at)) for at in range(1, bits, 2)]


def sent_blocks(part, me, first, count):
    blocks = part.reshape(1 << count, -1, LANES)
    mine = (me >> first) & ((1 << count) - 1)
    arrived = [
        exchange(lax.dynamic_index_in_dim(blocks, mine ^ m, 0, keepdims=False), m << first)
        for m in range(1, 1 << count)
    ]
    return [lax.dynamic_index_in_dim(blocks, mine, 0, keepdims=False)] + arrived


def added(blocks):
    total = blocks[0].astype(F32)
    for block in blocks[1:]:
        total = total + block.astype(F32)
    return total.astype(BF16)


def reduced(part, me, first, count):
    return added(sent_blocks(part, me, first, count))


def gathered(part, me, first, count):
    blocks = [part] + [exchange(part, m << first) for m in range(1, 1 << count)]
    for bit in range(count):
        swap = (me >> (first + bit)) & 1 == 1
        blocks = [jnp.where(swap, blocks[i ^ (1 << bit)], blocks[i]) for i in range(1 << count)]
    return jnp.concatenate(blocks, axis=0)


def shards(features, elem_owner, elem_voxel, w_first, b_first, w_conv, cotangent):
    n_brick = lax.axis_size("brick")
    devices = lax.axis_size(AXES)
    near = devices // 2
    me = lax.axis_index(AXES)
    rows, width = features.shape
    cap = 2 * rows // devices
    dims = cotangent.shape[1:4]
    half_x, half_y, half_z = dims
    cells = half_x * half_y * half_z
    vox_count = 8 * cells
    out_width = cotangent.shape[4]
    scale = 1.0 / math.sqrt(devices * cells)
    bias = b_first.reshape(1, width)
    offsets = w_conv.reshape(27, width, out_width)

    cot = cotangent.reshape(cells, out_width)
    plane = cotangent[0, :, :, 0, :].reshape(-1, out_width)
    above = passed_along(plane, "brick", -1)

    half = lax.axis_index("half").reshape(1)
    owner, voxel = elem_owner.reshape(1, rows), elem_voxel.reshape(1, rows)

    def swapped(packed):
        return lax.all_to_all(packed, ("dom", "brick"), split_axis=0, concat_axis=0, tiled=True)

    near_recv = swapped(pack(half, owner, voxel, features, cap, near, dims))
    far_packed = pack(1 - half, owner, voxel, features, cap, near, dims)
    far_recv = swapped(far_packed)

    n_conv = 27 * width
    unit = 2 * devices
    n_block = -(-(n_conv // 8 + (2 * width + PAD) // 8) // unit) * unit
    n_first = 8 * n_block - n_conv
    bit = (me & 1).reshape(1)
    near_codes = codes_of(near_recv, cap, vox_count)
    cots, near_codes = lax.optimization_barrier((jnp.concatenate([cot, above], axis=0), near_codes))
    far_cots = crossed(cots)
    near_out, near_edge, conv_term, *first_terms = slab(
        "near", bit, near_codes, near_recv, w_first, bias, cots, offsets, cap, scale, dims
    )
    far_codes = codes_of(far_recv, cap, vox_count)
    lent, rest, keep, send = slab(
        "far_ahead", bit, far_codes, far_recv, w_first, bias, far_cots, offsets, cap, scale, dims, (conv_term,)
    )
    lent, rest = crossed(lent), crossed(rest)
    part = added([keep, exchange(send, 1)])
    part, far_codes = lax.optimization_barrier((part, far_codes))
    groups = bit_groups()
    blocks = sent_blocks(part, me, *groups[1])
    first_part = slab(
        "far_back", bit, far_codes, far_recv, w_first, bias, far_cots, offsets, cap, scale, dims, first_terms, n_first
    )
    first_part, lent, blocks = lax.optimization_barrier((first_part, lent, blocks))
    for first, count in groups[:2]:
        first_part = reduced(first_part, me, first, count)
    part, first_part, rest = lax.optimization_barrier((added(blocks), first_part, rest))
    part = jnp.concatenate([part, first_part], axis=0)
    for first, count in groups[2:]:
        part = reduced(part, me, first, count)
    for first, count in reversed(groups[2:]):
        part = gathered(part, me, first, count)
    lent = jnp.concatenate([lent, rest], axis=0).astype(F32)
    part, edge = lax.optimization_barrier((part, near_edge + lent[cells:]))
    below = passed_along(edge, "brick", 1)
    part, below = lax.optimization_barrier((gathered(part, me, *groups[1]), below))
    conv_grad, w_first_grad, b_first_grad = finish(bit, part, exchange(part, 1), n_conv, width, scale)

    below = below.reshape(half_x, half_y, 1, out_width)
    whole = (near_out + lent[:cells]).reshape(half_x, half_y, half_z, out_width)
    volume_out = jnp.concatenate([whole[:, :, :1] + below, whole[:, :, 1:]], axis=2).astype(BF16)
    return (
        volume_out[None],
        conv_grad.reshape(w_conv.shape),
        w_first_grad,
        b_first_grad.reshape(width),
    )


def solution(mesh):
    n_dom, n_brick = mesh.devices.shape
    halves = jax.sharding.Mesh(mesh.devices.reshape(2, n_dom // 2, n_brick), AXES)
    bricks = P(("half", "dom"), None, None, "brick", None)
    return jax.shard_map(
        shards,
        mesh=halves,
        in_specs=(P(AXES, None), P(AXES, None), P(AXES), P(), P(), P(), bricks),
        out_specs=(bricks, P(), P(), P()),
        check_vma=False,
    )
```

```python
import functools
import math

import jax
import jax.numpy as jnp
from jax import lax
from jax.experimental import pallas as pl
from jax.experimental.pallas import tpu as pltpu
from jax.sharding import PartitionSpec as P

BF16 = jnp.bfloat16
F32 = jnp.float32
LANES = 128
PAD = 16
VMEM = pl.BlockSpec(memory_space=pltpu.VMEM)
BIG = 56 * 2**20
SMALL = 24 * 2**20
ANY = pl.BlockSpec(memory_space=pl.ANY)


def lasting(microseconds):
    return pl.CostEstimate(
        flops=int(microseconds * 1.1e9), bytes_accessed=int(microseconds * 3.5e6), transcendentals=0
    )


def dot(a, b):
    return jnp.dot(a, b, preferred_element_type=F32)


def dot_nt(a, b):
    return lax.dot_general(a, b, (((1,), (1,)), ((), ())), preferred_element_type=F32)


def dot_tn(a, b):
    return lax.dot_general(a, b, (((0,), (0,)), ((), ())), preferred_element_type=F32)


def shifts_of(parity):
    return [s for s in range(8) if s & ~parity == 0]


def offset_of(parity, shift):
    index = 0
    for bit in (4, 2, 1):
        index = 3 * index + (1 if not parity & bit else 0 if shift & bit else 2)
    return index


def pack_kernel(group, cap, dims, half_ref, owner_ref, voxel_ref, feat_ref, out_ref, slot_ref, table_ref):
    rows = feat_ref.shape[0]
    devices = table_ref.shape[0] // 2
    half_x, half_y, half_z = dims
    cells = half_x * half_y * half_z
    first_device = half_ref[0] * devices
    step = 2 * LANES

    @pl.when(pl.program_id(0) == 0)
    def _():
        before = lax.broadcasted_iota(jnp.int32, (step, step), 0) < lax.broadcasted_iota(
            jnp.int32, (step, step), 1
        )
        before = before.astype(F32).astype(BF16)
        device = lax.broadcasted_iota(jnp.int32, (devices, step), 0)
        place = lax.broadcasted_iota(jnp.int32, (LANES, step), 0).astype(F32)
        seen = jnp.zeros((devices, 1), F32)
        table = jnp.zeros((2 * devices, LANES), F32)
        for start in range(0, rows, step):
            here = (device == owner_ref[:, start : start + step] - first_device).astype(F32)
            rank = here * (dot(here.astype(BF16), before) + seen + 1.0)
            slot = jnp.sum(rank + here * (device * cap).astype(F32), axis=0, keepdims=True) - 1.0
            slot_ref[:, start : start + step] = slot.astype(jnp.int32)
            seen = seen + jnp.sum(here, axis=1, keepdims=True)
            voxel = voxel_ref[:, start : start + step]
            z, line = voxel % (2 * half_z), voxel // (2 * half_z)
            y, x = line % (2 * half_y), line // (2 * half_y)
            parity = (x % 2) * 4 + (y % 2) * 2 + z % 2
            code = parity * cells + ((x // 2) * half_y + y // 2) * half_z + z // 2
            high, low = (code >> 7) + 1, code & 127
            values = jnp.concatenate([here * high.astype(F32), here * low.astype(F32)], axis=0)
            ranked = jnp.where(place == jnp.sum(rank, axis=0, keepdims=True) - 1.0, 1.0, 0.0)
            table = table + dot_nt(values.astype(BF16), ranked.astype(BF16))
        table_ref[...] = table

    first = pl.program_id(0) * group
    place = lax.broadcasted_iota(jnp.int32, (group * cap, rows), 0) + first * cap
    chosen = jnp.where(place == slot_ref[...], 1.0, 0.0).astype(BF16)
    packed = dot(chosen, feat_ref[...]).astype(BF16)
    for g in range(group):
        out_ref[g, :cap, :] = packed[g * cap : (g + 1) * cap]
        high = table_ref[pl.ds(first + g, 1), :]
        low = table_ref[pl.ds(devices + first + g, 1), :]
        both = jnp.concatenate([high, low], axis=1)
        out_ref[g, cap:, :] = jnp.broadcast_to(both, (PAD, 2 * LANES)).astype(BF16)


def pack(half, owner, voxel, features, cap, devices, dims):
    rows, width = features.shape
    group = max(1, 512 // cap)
    return pl.pallas_call(
        functools.partial(pack_kernel, group, cap, dims),
        out_shape=jax.ShapeDtypeStruct((devices, cap + PAD, width), BF16),
        grid_spec=pltpu.PrefetchScalarGridSpec(
            num_scalar_prefetch=1,
            grid=(devices // group,),
            in_specs=[VMEM] * 3,
            out_specs=pl.BlockSpec((group, cap + PAD, width), lambda i, half: (i, 0, 0)),
            scratch_shapes=[pltpu.VMEM((1, rows), jnp.int32), pltpu.VMEM((2 * devices, LANES), F32)],
        ),
        compiler_params=pltpu.CompilerParams(vmem_limit_bytes=BIG),
        cost_estimate=lasting(4),
        name="pack",
    )(half, owner, voxel, features)


def lay_out(cot_ref, dims, wide, tall):
    half_x, half_y, half_z = dims
    cells = half_x * half_y * half_z
    width = cot_ref.shape[1]
    same = cot_ref[:cells, :].astype(F32)
    above = jnp.broadcast_to(cot_ref[cells:, :].astype(F32)[:, None, :], (cells // half_z, half_z, width))
    highest = lax.broadcasted_iota(jnp.int32, (cells, width), 0) % half_z == half_z - 1
    ahead = jnp.where(highest, above.reshape(cells, width), pltpu.roll(same, cells - 1, 0))
    for shift in range(8):
        values = ahead if shift & 1 else same
        if shift & 4:
            gap = half_y * half_z
            values = jnp.concatenate([values[gap:], jnp.zeros((gap, width), F32)], axis=0)
        if shift & 2:
            values = values.reshape(half_x, half_y * half_z, width)
            gone = jnp.zeros((half_x, half_z, width), F32)
            values = jnp.concatenate([values[:, half_z:], gone], axis=1).reshape(cells, width)
        if wide is not None:
            wide[:, shift * width : (shift + 1) * width] = values.astype(BF16)
        if tall is not None:
            tall[shift * width : (shift + 1) * width, :] = values.T.astype(BF16)


def codes_of(recv, cap, vox_count):
    parts = recv[:, cap, :].astype(jnp.int32)
    high, low = parts[:, :cap], parts[:, LANES : LANES + cap]
    return jnp.where(high > 0, (high - 1) * 128 + low, vox_count).reshape(-1)


def put_rows(ref, start, values):
    count = values.shape[0]
    ref[pl.ds(2 * start, count, stride=2), :] = values[:, :LANES]
    ref[pl.ds(2 * start + 1, count, stride=2), :] = values[:, LANES:]


def get_rows(ref, start, count):
    low = ref[pl.ds(2 * start, count, stride=2), :]
    high = ref[pl.ds(2 * start + 1, count, stride=2), :]
    return low, high


UNROLL = 16
CHUNK = 1024


def pairs_of(ref):
    return ref.reshape(ref.shape[0] // 2, 2, LANES)


def add_products(block, conv_ref, parity, dims, same, next_):
    half_x, half_y, half_z = dims
    plane = half_y * half_z
    width = conv_ref.shape[2]
    shifts = shifts_of(parity)
    right = jnp.concatenate([conv_ref[offset_of(parity, s)] for s in shifts], axis=1)
    product = dot(block, right)
    for at, s in enumerate(shifts):
        part = product[:, at * width : (at + 1) * width].reshape(half_x, plane, width)
        dx = 1 if s & 4 else 0
        dy = half_z if s & 2 else 0
        total = next_ if s & 1 else same
        total[dx:, dy:, :] += part[: half_x - dx, : plane - dy, :]


def shifted_along_z(same, next_, dims):
    half_x, half_y, half_z = dims
    cells = half_x * half_y * half_z
    width = same.shape[2]
    after = next_[...].reshape(cells, width)
    lowest = lax.broadcasted_iota(jnp.int32, (cells, width), 0) % half_z == 0
    total = same[...].reshape(cells, width) + jnp.where(lowest, 0.0, pltpu.roll(after, 1, 0))
    return total, after.reshape(cells // half_z, half_z, width)[:, half_z - 1, :]


def slab_kernel(cap, scale, dims, kind, *refs):
    ahead, back, far = kind != "far_back", kind != "far_ahead", kind != "near"
    bit, codes, recv_ref, w_ref, b_ref, cot_ref, conv_hbm = refs[:7]
    wide = tall = slopes = None
    if kind == "near":
        out_ref, edge_ref, terms_hbm, wgrad, bgrad, sums, rows, conv, sems, slopes, wide, tall, terms, same, next_ = refs[7:]
    elif kind == "far_ahead":
        terms_hbm, lent_ref, rest_ref, keep_hbm, send_hbm, sums, rows, conv, sems, tall, terms, flat, same, next_ = refs[7:]
    else:
        wterm_ref, bterm_ref, first_ref, sums, rows, conv, sems, slopes, wide, wgrad, bgrad = refs[7:]
    sources, _, width = recv_ref.shape
    half_x, half_y, half_z = dims
    cells = half_x * half_y * half_z
    vox_count = 8 * cells
    out_width = conv.shape[2]
    count = sources * cap
    loads = [pltpu.make_async_copy(conv_hbm, conv, sems.at[0])]
    if kind == "far_ahead":
        loads.append(pltpu.make_async_copy(terms_hbm, terms, sems.at[1]))
    for load in loads:
        load.start()
    lay_out(cot_ref, dims, wide, tall)
    step = CHUNK // cap
    sum_rows, new_rows = pairs_of(sums), pairs_of(rows)

    def layer(i, _):
        feats = recv_ref[pl.ds(i * step, step), :cap, :].reshape(CHUNK, width)
        pre = dot(feats, w_ref[...]) + b_ref[...]
        sig = jax.nn.sigmoid(pre)
        if ahead:
            put_rows(rows, i * CHUNK, (pre * sig).astype(BF16).astype(F32))
        if back:
            slopes[pl.ds(i * CHUNK, CHUNK), :] = sig * (1.0 + pre * (1.0 - sig))
        return 0

    lax.fori_loop(0, count // CHUNK, layer, 0)
    if ahead:

        def clear(i, _):
            sums[pl.ds(pl.multiple_of(i * 1024, 1024), 1024), :] = jnp.zeros((1024, LANES), F32)
            return 0

        lax.fori_loop(0, vox_count // 512, clear, 0)

        def add(i, _):
            for u in range(0, UNROLL, 2):
                at = i * UNROLL + u
                a, b = codes[at], codes[at + 1]
                old_a, old_b = sum_rows[a], sum_rows[b]
                new_a = old_a + new_rows[at]
                new_b = jnp.where(a == b, new_a, old_b) + new_rows[at + 1]
                sum_rows[a] = new_a
                sum_rows[b] = new_b
            return 0

        lax.fori_loop(0, count // UNROLL, add, 0)
    for load in loads:
        load.wait()
    if ahead:
        same[...] = jnp.zeros_like(same)
        next_[...] = jnp.zeros_like(next_)
    stores = []
    for parity in range(8):
        shifts = shifts_of(parity)
        if ahead:
            low, high = get_rows(sums, parity * cells, cells)
            block = jnp.concatenate([low.astype(BF16), high.astype(BF16)], axis=1)
            left = jnp.concatenate([tall[s * out_width : (s + 1) * out_width, :] for s in shifts], axis=0)
            grads = dot(left, block)
            for at, s in enumerate(shifts):
                first = offset_of(parity, s) * width
                grad = grads[at * out_width : (at + 1) * out_width].T
                if far:
                    flat[first : first + width, :] = (grad + terms[first : first + width, :]).astype(BF16)
                else:
                    terms[first : first + width, :] = grad
            add_products(block, conv, parity, dims, same, next_)
        if back:
            left = jnp.concatenate([wide[:, s * out_width : (s + 1) * out_width] for s in shifts], axis=1)
            right = jnp.concatenate([conv[offset_of(parity, s)] for s in shifts], axis=1)
            put_rows(sums, parity * cells, (dot_nt(left, right) * scale).astype(BF16).astype(F32))
    if kind == "near":
        out_ref[...], edge_ref[...] = shifted_along_z(same, next_, dims)
        stores.append(pltpu.make_async_copy(terms, terms_hbm, sems.at[1]))
        stores[-1].start()
    if kind == "far_ahead":
        size = flat.shape[0] // 2
        mine = pl.multiple_of(bit[0] * size, 16)
        other = pl.multiple_of((1 - bit[0]) * size, 16)
        stores = [
            pltpu.make_async_copy(flat.at[pl.ds(mine, size)], keep_hbm, sems.at[2]),
            pltpu.make_async_copy(flat.at[pl.ds(other, size)], send_hbm, sems.at[3]),
        ]
        for store in stores:
            store.start()
        total, edge = shifted_along_z(same, next_, dims)
        cut = lent_ref.shape[0]
        lent_ref[...] = total[:cut].astype(BF16)
        rest_ref[: cells - cut, :] = total[cut:].astype(BF16)
        rest_ref[cells - cut :, :] = edge.astype(BF16)
    if back:
        sums[2 * vox_count :, :] = jnp.zeros((16, LANES), F32)

        def take(i, _):
            for u in range(UNROLL):
                at = i * UNROLL + u
                new_rows[at] = sum_rows[codes[at]]
            return 0

        lax.fori_loop(0, count // UNROLL, take, 0)
        wgrad[...] = wterm_ref[...] if far else jnp.zeros_like(wgrad)
        bgrad[...] = bterm_ref[...] if far else jnp.zeros_like(bgrad)

        def layer_back(i, _):
            feats = recv_ref[pl.ds(i * step, step), :cap, :].reshape(CHUNK, width)
            low, high = get_rows(rows, i * CHUNK, CHUNK)
            pre_grad = (jnp.concatenate([low, high], axis=1) * slopes[pl.ds(i * CHUNK, CHUNK), :]).astype(BF16)
            wgrad[...] += dot_tn(feats, pre_grad)
            bgrad[...] += jnp.sum(pre_grad.astype(F32), axis=0, keepdims=True)
            return 0

        lax.fori_loop(0, count // CHUNK, layer_back, 0)
    if kind == "far_back":
        first_ref[:width, :] = wgrad[:, :LANES].astype(BF16)
        first_ref[width : 2 * width, :] = wgrad[:, LANES:].astype(BF16)
        bias = bgrad[...]
        row = lax.broadcasted_iota(jnp.int32, (PAD, LANES), 0)
        bias = jnp.where(row == 0, bias[:, :LANES], jnp.where(row == 1, bias[:, LANES:], 0.0))
        first_ref[2 * width : 2 * width + PAD, :] = bias.astype(BF16)
        rest = first_ref.shape[0] - 2 * width - PAD
        first_ref[2 * width + PAD :, :] = jnp.zeros((rest, LANES), BF16)
    for store in stores:
        store.wait()


def slab(kind, bit, codes, recv, w_first, b_first, cot, w_conv, cap, scale, dims, earlier=(), length=None):
    sources, _, width = recv.shape
    half_x, half_y, half_z = dims
    cells = half_x * half_y * half_z
    out_width = w_conv.shape[2]
    n_conv = 27 * width
    count = sources * cap
    operands = (recv, w_first, b_first, cot, w_conv) + tuple(earlier)
    in_specs = [VMEM] * 4 + [ANY]
    scratch = [
        pltpu.VMEM((2 * 8 * cells + 16, LANES), F32),
        pltpu.VMEM((2 * count, LANES), F32),
        pltpu.VMEM(w_conv.shape, BF16),
        pltpu.SemaphoreType.DMA((4,)),
    ]
    slopes = pltpu.VMEM((count, width), F32)
    wide = pltpu.VMEM((cells, 8 * out_width), BF16)
    tall = pltpu.VMEM((8 * out_width, cells), BF16)
    terms = pltpu.VMEM((n_conv, LANES), F32)
    outputs = [pltpu.VMEM((half_x, half_y * half_z, out_width), F32)] * 2
    first_layer = (jax.ShapeDtypeStruct((width, width), F32), jax.ShapeDtypeStruct((1, width), F32))
    if kind == "near":
        out_shape = (
            jax.ShapeDtypeStruct((cells, out_width), F32),
            jax.ShapeDtypeStruct((cells // half_z, out_width), F32),
            jax.ShapeDtypeStruct((n_conv, LANES), F32),
        ) + first_layer
        out_specs = (VMEM, VMEM, ANY, VMEM, VMEM)
        scratch += [slopes, wide, tall, terms] + outputs
    elif kind == "far_ahead":
        in_specs += [ANY]
        lent = (cells + cells // half_z) * 11 // 16
        out_shape = (
            jax.ShapeDtypeStruct((lent, out_width), BF16),
            jax.ShapeDtypeStruct((cells + cells // half_z - lent, out_width), BF16),
            jax.ShapeDtypeStruct((n_conv // 2, LANES), BF16),
            jax.ShapeDtypeStruct((n_conv // 2, LANES), BF16),
        )
        out_specs = (VMEM, VMEM, ANY, ANY)
        scratch += [tall, terms, pltpu.VMEM((n_conv, LANES), BF16)]
        scratch += outputs
    else:
        in_specs += [VMEM, VMEM]
        out_shape = jax.ShapeDtypeStruct((length, LANES), BF16)
        out_specs = VMEM
        scratch += [slopes, wide, pltpu.VMEM((width, width), F32), pltpu.VMEM((1, width), F32)]
    return pl.pallas_call(
        functools.partial(slab_kernel, cap, scale, dims, kind),
        out_shape=out_shape,
        grid_spec=pltpu.PrefetchScalarGridSpec(
            num_scalar_prefetch=2, grid=(1,), in_specs=in_specs, out_specs=out_specs, scratch_shapes=scratch
        ),
        compiler_params=pltpu.CompilerParams(vmem_limit_bytes=BIG),
        cost_estimate=lasting({"near": 26, "far_ahead": 20, "far_back": 11}[kind]),
        name="slab_" + kind,
    )(bit, codes, *operands)


def finish_kernel(scale, n_block, bit_ref, mine_ref, theirs_ref, conv_ref, w_ref, b_ref, first):
    width = w_ref.shape[0]
    n_conv = conv_ref.shape[0] // 8
    n_first = n_block - n_conv

    def write(refs):
        for k in range(8):
            source, at = refs[k // 4], k % 4 * n_block
            conv_ref[k * n_conv : (k + 1) * n_conv, :] = source[at : at + n_conv, :].astype(F32) * scale
            first[k * n_first : (k + 1) * n_first, :] = source[at + n_conv : at + n_block, :].astype(F32)
        w_ref[:, :LANES] = first[:width, :]
        w_ref[:, LANES:] = first[width : 2 * width, :]
        bias = first[2 * width : 2 * width + 8, :]
        b_ref[...] = jnp.concatenate([bias[0:1], bias[1:2]], axis=1)

    @pl.when(bit_ref[0] == 0)
    def _():
        write((mine_ref, theirs_ref))

    @pl.when(bit_ref[0] == 1)
    def _():
        write((theirs_ref, mine_ref))


def finish(bit, mine, theirs, n_conv, width, scale):
    n_block = mine.shape[0] // 4
    return pl.pallas_call(
        functools.partial(finish_kernel, scale, n_block),
        out_shape=(
            jax.ShapeDtypeStruct((n_conv, LANES), F32),
            jax.ShapeDtypeStruct((width, width), F32),
            jax.ShapeDtypeStruct((1, width), F32),
        ),
        grid_spec=pltpu.PrefetchScalarGridSpec(
            num_scalar_prefetch=1,
            grid=(1,),
            in_specs=[VMEM] * 2,
            out_specs=(VMEM,) * 3,
            scratch_shapes=[pltpu.VMEM((8 * n_block - n_conv, LANES), F32)],
        ),
        compiler_params=pltpu.CompilerParams(vmem_limit_bytes=SMALL),
        cost_estimate=lasting(3),
        name="finish",
    )(bit, mine, theirs)


AXES = ("half", "dom", "brick")


def passed_along(array, axis, by):
    size = lax.axis_size(axis)
    pairs = [(i, i + by) for i in range(size) if 0 <= i + by < size]
    return lax.ppermute(array, axis, pairs)


def crossed(array):
    return lax.ppermute(array, "half", [(0, 1), (1, 0)])


def exchange(array, mask):
    return lax.ppermute(array, AXES, [(i, i ^ mask) for i in range(lax.axis_size(AXES))])


def bit_groups():
    bits = lax.axis_size(AXES).bit_length() - 1
    return [(0, 1)] + [(at, min(2, bits - at)) for at in range(1, bits, 2)]


def sent_blocks(part, me, first, count):
    blocks = part.reshape(1 << count, -1, LANES)
    mine = (me >> first) & ((1 << count) - 1)
    arrived = [
        exchange(lax.dynamic_index_in_dim(blocks, mine ^ m, 0, keepdims=False), m << first)
        for m in range(1, 1 << count)
    ]
    return [lax.dynamic_index_in_dim(blocks, mine, 0, keepdims=False)] + arrived


def added(blocks):
    total = blocks[0].astype(F32)
    for block in blocks[1:]:
        total = total + block.astype(F32)
    return total.astype(BF16)


def reduced(part, me, first, count):
    return added(sent_blocks(part, me, first, count))


def gathered(part, me, first, count):
    blocks = [part] + [exchange(part, m << first) for m in range(1, 1 << count)]
    for bit in range(count):
        swap = (me >> (first + bit)) & 1 == 1
        blocks = [jnp.where(swap, blocks[i ^ (1 << bit)], blocks[i]) for i in range(1 << count)]
    return jnp.concatenate(blocks, axis=0)


def shards(features, elem_owner, elem_voxel, w_first, b_first, w_conv, cotangent):
    n_brick = lax.axis_size("brick")
    devices = lax.axis_size(AXES)
    near = devices // 2
    me = lax.axis_index(AXES)
    rows, width = features.shape
    cap = 2 * rows // devices
    dims = cotangent.shape[1:4]
    half_x, half_y, half_z = dims
    cells = half_x * half_y * half_z
    vox_count = 8 * cells
    out_width = cotangent.shape[4]
    scale = 1.0 / math.sqrt(devices * cells)
    bias = b_first.reshape(1, width)
    offsets = w_conv.reshape(27, width, out_width)

    cot = cotangent.reshape(cells, out_width)
    plane = cotangent[0, :, :, 0, :].reshape(-1, out_width)
    above = passed_along(plane, "brick", -1)

    half = lax.axis_index("half").reshape(1)
    owner, voxel = elem_owner.reshape(1, rows), elem_voxel.reshape(1, rows)

    def swapped(packed):
        return lax.all_to_all(packed, ("dom", "brick"), split_axis=0, concat_axis=0, tiled=True)

    near_recv = swapped(pack(half, owner, voxel, features, cap, near, dims))
    far_packed = pack(1 - half, owner, voxel, features, cap, near, dims)
    far_recv = swapped(far_packed)

    n_conv = 27 * width
    unit = 2 * devices
    n_block = -(-(n_conv // 8 + (2 * width + PAD) // 8) // unit) * unit
    n_first = 8 * n_block - n_conv
    bit = (me & 1).reshape(1)
    near_codes = codes_of(near_recv, cap, vox_count)
    cots, near_codes = lax.optimization_barrier((jnp.concatenate([cot, above], axis=0), near_codes))
    far_cots = crossed(cots)
    near_out, near_edge, conv_term, *first_terms = slab(
        "near", bit, near_codes, near_recv, w_first, bias, cots, offsets, cap, scale, dims
    )
    far_codes = codes_of(far_recv, cap, vox_count)
    lent, rest, keep, send = slab(
        "far_ahead", bit, far_codes, far_recv, w_first, bias, far_cots, offsets, cap, scale, dims, (conv_term,)
    )
    lent, rest = crossed(lent), crossed(rest)
    part = added([keep, exchange(send, 1)])
    part, far_codes = lax.optimization_barrier((part, far_codes))
    groups = bit_groups()
    blocks = sent_blocks(part, me, *groups[1])
    first_part = slab(
        "far_back", bit, far_codes, far_recv, w_first, bias, far_cots, offsets, cap, scale, dims, first_terms, n_first
    )
    first_part, lent, blocks = lax.optimization_barrier((first_part, lent, blocks))
    for first, count in groups[:2]:
        first_part = reduced(first_part, me, first, count)
    part, first_part, rest = lax.optimization_barrier((added(blocks), first_part, rest))
    part = jnp.concatenate([part, first_part], axis=0)
    for first, count in groups[2:]:
        part = reduced(part, me, first, count)
    for first, count in reversed(groups[2:]):
        part = gathered(part, me, first, count)
    lent = jnp.concatenate([lent, rest], axis=0).astype(F32)
    part, edge = lax.optimization_barrier((part, near_edge + lent[cells:]))
    below = passed_along(edge, "brick", 1)
    part, below = lax.optimization_barrier((gathered(part, me, *groups[1]), below))
    conv_grad, w_first_grad, b_first_grad = finish(bit, part, exchange(part, 1), n_conv, width, scale)

    below = below.reshape(half_x, half_y, 1, out_width)
    whole = (near_out + lent[:cells]).reshape(half_x, half_y, half_z, out_width)
    volume_out = jnp.concatenate([whole[:, :, :1] + below, whole[:, :, 1:]], axis=2).astype(BF16)
    return (
        volume_out[None],
        conv_grad.reshape(w_conv.shape),
        w_first_grad,
        b_first_grad.reshape(width),
    )


def solution(mesh):
    n_dom, n_brick = mesh.devices.shape
    halves = jax.sharding.Mesh(mesh.devices.reshape(2, n_dom // 2, n_brick), AXES)
    bricks = P(("half", "dom"), None, None, "brick", None)
    return jax.shard_map(
        shards,
        mesh=halves,
        in_specs=(P(AXES, None), P(AXES, None), P(AXES), P(), P(), P(), bricks),
        out_specs=(bricks, P(), P(), P()),
        check_vma=False,
    )
```
